256 devices in a mesh: query: 8 (over x_hi, y), passage: 32 (over z, x_lo, core).
Axes of the slice: x: 4 (x_hi: 2, x_lo: 2; x = x_hi * 2 + x_lo), y: 4, z: 8, core: 2. Of those that a mesh axis runs over, the one named last changes fastest.
Arguments:
- queries: bfloat16 [32768, 4096], P(('query', 'passage')), may hold values from -32 to 32
- passages: bfloat16 [1024, 4096], P('passage'), may hold values from -8 to 8
- candidates: int32 [32768, 128], P(('query', 'passage')), may hold values from 0 to 1023, as said below
- teacher_scores: float32 [32768, 128], P(('query', 'passage')), may hold values from -20 to 260
Outputs:
- query_loss: float32 [32768], P(('query', 'passage'))
- grad_queries: float32 [32768, 4096], P(('query', 'passage'))
- grad_passages: float32 [1024, 4096], P('passage', 'query')
The draws below stay inside these ranges and needn't reach their ends.
Inputs may be any that keep to these rules, and one draw needn't show every extreme that they name: Each row holds 128 different indices in rising order, so that a query's candidates come grouped by the passage shard that holds them; some shards of the pool are named far more often than others.
All inputs are finite; a program needn't handle non-finite values.
Results may differ from the reference program's by a relative error of at most 0.0028.
Values may be sent and summed in bfloat16 or wider, within the bound.
A program may use at most 128 MiB of HBM per device.

```python
import math
import jax
import jax.numpy as jnp
from jax import lax

E = 4096
W1 = 64
W2 = 256
W3 = 1024
K = 128
PASSAGE_SPAN = 32
QUERIES = 32768
PASSAGE_COUNT = 1024
N_PASSAGE = 32


def pool_values(key):
    pool_key = jax.random.fold_in(key, 101)
    normal_key = jax.random.fold_in(pool_key, 0)
    normal_part = jnp.clip(jax.random.normal(normal_key, (PASSAGE_COUNT, E), jnp.float32), -4.0, 4.0)
    return normal_part


def candidate_ids(key):
    identity_key = jax.random.fold_in(key, 202)
    baseline_key, boost_key = jax.random.split(identity_key)
    baseline_scores = jax.random.randint(baseline_key, (QUERIES, PASSAGE_COUNT), 0, 4096)
    extra_boost = jax.random.randint(boost_key, (N_PASSAGE,), 0, 1024)
    boosted_rows = jnp.repeat(extra_boost, PASSAGE_SPAN)
    relevance_score = (baseline_scores + boosted_rows[None, :]) * PASSAGE_COUNT + jnp.arange(PASSAGE_COUNT, dtype=jnp.int32)[None, :]
    best, chosen = lax.top_k(relevance_score, K)
    return jnp.sort(chosen, axis=1).astype(jnp.int32)


def draw_passages(key, part):
    pool = pool_values(key)
    return pool.astype(jnp.bfloat16)


def draw_candidates(key, part):
    return candidate_ids(key)


def draw_queries(key, part):
    key = jax.random.fold_in(key, 7)
    baseline_key = jax.random.fold_in(key, 0)
    values = jnp.clip(jax.random.normal(baseline_key, (QUERIES, E), jnp.float32), -6.0, 6.0)
    return jnp.clip(values, -32.0, 32.0).astype(jnp.bfloat16)


def draw_teacher_scores(key, part):
    key = jax.random.fold_in(key, 13)
    baseline_key = jax.random.fold_in(key, 0)
    return jnp.clip(3.0 * jax.random.normal(baseline_key, (QUERIES, K), jnp.float32), -18.0, 18.0)


def setup_inputs(seed: int = 0) -> dict:
    streams_of = jax.random.split(jax.random.key(seed), 5)
    return {
        "queries": draw_queries(jax.random.fold_in(streams_of[4], 71), 0),
        "passages": draw_passages(jax.random.fold_in(streams_of[4], 71), 0),
        "candidates": draw_candidates(jax.random.fold_in(streams_of[4], 71), 0),
        "teacher_scores": draw_teacher_scores(jax.random.fold_in(streams_of[4], 71), 0),
    }


def segment_bounds(full_width):
    return (0, W1, W2, W3, full_width)

def piece_logits(query_rows, shard_rows, first_row, chosen):
    bounds = segment_bounds(query_rows.shape[1])
    products = []
    for segment in range(4):
        lower, upper = (bounds[segment], bounds[segment + 1])
        products.append(jnp.dot(query_rows[:, lower:upper], shard_rows[:, lower:upper].T, preferred_element_type=jnp.float32))
    running = products[0]
    levels = [running]
    for segment in range(1, 4):
        running = running + products[segment]
        levels.append(running)
    stacked = jnp.stack(levels)
    offset = chosen - first_row
    inside = (offset >= 0) & (offset < shard_rows.shape[0])
    clipped = jnp.clip(offset, 0, shard_rows.shape[0] - 1).astype(jnp.int32)
    picked = jnp.take_along_axis(stacked, jnp.broadcast_to(clipped[None], (4,) + clipped.shape), axis=2)
    return jnp.where(inside[None], picked, jnp.zeros_like(picked))

def head_terms(logits, scores, full_width):
    widths = (W1, W2, W3, full_width)
    scales = jnp.array([1.0 / math.sqrt(value) for value in widths], jnp.float32)[:, None, None]
    log_teacher = jax.nn.log_softmax(scores, axis=-1)
    teacher = jnp.exp(log_teacher)
    student = jax.nn.log_softmax(logits * scales, axis=-1)
    query_loss = lax.optimization_barrier(jnp.sum(teacher[None] * (log_teacher[None] - student), axis=(0, 2)))
    dlogit = (jnp.exp(student) - teacher[None]) * scales
    tail_two = dlogit[2] + dlogit[3]
    tail_one = dlogit[1] + tail_two
    coefficient = jnp.stack([dlogit[0] + tail_one, tail_one, tail_two, dlogit[3]]).astype(jnp.bfloat16)
    return (query_loss, coefficient)

def spread_grid(coefficient, chosen, pool_size):
    row_ids = jnp.broadcast_to(jnp.arange(chosen.shape[0], dtype=jnp.int32)[:, None], chosen.shape)
    empty = jnp.zeros((4, chosen.shape[0], pool_size), jnp.bfloat16)
    return empty.at[:, row_ids, chosen].set(coefficient)

def query_gradient(accumulated, grid, shard_rows, first_row):
    bounds = segment_bounds(accumulated.shape[1])
    window = lax.dynamic_slice_in_dim(grid, first_row, shard_rows.shape[0], 2)
    products = []
    for segment in range(4):
        lower, upper = (bounds[segment], bounds[segment + 1])
        products.append(jnp.dot(window[segment], shard_rows[:, lower:upper], preferred_element_type=jnp.float32))
    return accumulated + jnp.concatenate(products, axis=1)

def passage_term(grid, query_rows, first_row, row_count):
    bounds = segment_bounds(query_rows.shape[1])
    window = lax.dynamic_slice_in_dim(grid, first_row, row_count, 2)
    products = []
    for segment in range(4):
        lower, upper = (bounds[segment], bounds[segment + 1])
        products.append(jnp.dot(window[segment].T, query_rows[:, lower:upper], preferred_element_type=jnp.float32))
    return jnp.concatenate(products, axis=1)

def reference(queries, passages, candidates, teacher_scores):
    pool_size = passages.shape[0]
    full_width = queries.shape[1]
    window = 128
    block_count = queries.shape[0] // window
    query_blocks = queries.reshape(block_count, window, full_width)
    chosen_blocks = candidates.reshape(block_count, window, candidates.shape[1])
    score_blocks = teacher_scores.reshape(block_count, window, teacher_scores.shape[1])

    def step(accumulated, inputs):
        query_rows, chosen, scores = inputs
        logits = piece_logits(query_rows, passages, 0, chosen)
        query_loss, coefficient = head_terms(logits, scores, full_width)
        grid = spread_grid(coefficient, chosen, pool_size)
        grad_rows = query_gradient(jnp.zeros((window, full_width), jnp.float32), grid, passages, 0)
        accumulated = accumulated + passage_term(grid, query_rows, 0, pool_size)
        return (accumulated, (query_loss, grad_rows))
    total, (losses, grads) = lax.scan(step, jnp.zeros((pool_size, full_width), jnp.float32), (query_blocks, chosen_blocks, score_blocks))
    return (losses.reshape(-1), grads.reshape(-1, full_width), total)
```

```python
import functools
import math

import jax
import jax.numpy as jnp
from jax import lax
from jax.experimental import pallas as pl
from jax.experimental.pallas import tpu as pltpu
from jax.sharding import PartitionSpec as P

MESH = pl.DeviceIdType.MESH
BF16 = jnp.bfloat16
F32 = jnp.float32

E = 4096
W1, W2, W3 = 64, 256, 1024
WIDTHS = (W1, W2, W3, E)
ROWS = 128
SPAN = 32
HALF = 16
NX, NY, NZ = 4, 4, 8
POOL = 2 * NZ * SPAN
GROUP = NZ * SPAN
LANES = 128
BIG = 3.0e38

QUARTER = 384
FLAT = E - 4 * QUARTER

BLOCK = 512
WA = 256
WB = BLOCK - WA


def place():
    query = lax.axis_index("query")
    passage = lax.axis_index("passage")
    x = (query // 4) * 2 + (passage // 2) % 2
    return x, query % 4, passage // 4, passage % 2


def device(x, y, z, core):
    x, y, z = x % NX, y % NY, z % NZ
    return ((x // 2) * 4 + y, (z * 2 + x % 2) * 2 + core)


def prep_kernel(candidates, scores, dense, entropy):
    x, y, z, core = place()
    raw = scores[...]
    shifted = raw - jnp.max(raw, axis=1, keepdims=True)
    log_teacher = shifted - jnp.log(jnp.sum(jnp.exp(shifted), axis=1, keepdims=True))
    teacher = jnp.exp(log_teacher)
    entropy[...] = jnp.broadcast_to(
        jnp.sum(teacher * log_teacher, axis=1, keepdims=True), (ROWS, LANES)
    )
    chosen = candidates[...]
    lane = lax.broadcasted_iota(jnp.int32, (ROWS, LANES), 1)
    for half in range(2):
        for chunk in range(POOL // LANES):
            slot = lane // SPAN + chunk * (LANES // SPAN)
            dxl, dz = slot // NZ, slot % NZ
            owner = (((z + dz) % NZ) * 2 + (x + dxl) % 2) * 2 + half
            target = owner * SPAN + lane % SPAN
            position = jnp.zeros((ROWS, LANES), jnp.int32)
            for step in (64, 32, 16, 8, 4, 2, 1):
                probe = jnp.take_along_axis(chosen, position + (step - 1), axis=1)
                position = jnp.where(probe < target, position + step, position)
            hit = jnp.take_along_axis(chosen, position, axis=1) == target
            value = jnp.take_along_axis(teacher, position, axis=1)
            dense[half, :, chunk * LANES : (chunk + 1) * LANES] = jnp.where(hit, value, -1.0)


def prepare(candidates, scores):
    return pl.pallas_call(
        prep_kernel,
        out_shape=(
            jax.ShapeDtypeStruct((2, ROWS, POOL), F32),
            jax.ShapeDtypeStruct((ROWS, LANES), F32),
        ),
        in_specs=[pl.BlockSpec(memory_space=pltpu.VMEM)] * 2,
        out_specs=(pl.BlockSpec(memory_space=pltpu.VMEM),) * 2,
        name="prepare",
    )(candidates, scores)


SCRATCH = dict(
    qs=((2 * ROWS, E), BF16),
    ws=((2 * GROUP, E), BF16),
    tt=((2 * ROWS, POOL), F32),
    lv=((4, 2 * ROWS, POOL), F32),
    st=((2 * ROWS, LANES), F32),
    sr=((2 * ROWS, LANES), F32),
    grid=((4, 2 * ROWS, POOL), BF16),
    go=((ROWS, E), F32),
    gs=((ROWS, E), F32),
    gr=((ROWS, E), F32),
    pa=((NZ, 2, 8, SPAN, WA), F32),
    pab=((NZ, 2, 8, SPAN, WA), BF16),
    ra=((2, 4, 2, 8, SPAN, WA), BF16),
    fa=((2, 2, 4, SPAN, WA), F32),
    rax=((3, 4, SPAN, WA), F32),
    ga=((4, SPAN, WA), F32),
    ray=((3, SPAN, WA), F32),
    pb=((2, 2, 4, NZ, HALF, WB), F32),
    pbb=((2, 2, 4, NZ, HALF, WB), BF16),
    rbx=((3, 4, NZ, HALF, WB), BF16),
    gb=((4, NZ, HALF, WB), F32),
    gbb=((4, NZ, HALF, WB), BF16),
    rby=((3, NZ, HALF, WB), BF16),
    hb=((NZ, HALF, WB), F32),
    rbz=((7, HALF, WB), F32),
    pc=((4, 2, 2, NZ, HALF, WB), F32),
    pcb=((4, 2, 2, NZ, HALF, WB), BF16),
    rcy=((3, 2, 2, NZ, HALF, WB), BF16),
    gc=((2, 2, NZ, HALF, WB), F32),
    gcb=((2, 2, NZ, HALF, WB), BF16),
    rcx=((3, NZ, HALF, WB), BF16),
    hc=((NZ, HALF, WB), F32),
    rcz=((7, HALF, WB), F32),
    ob=((SPAN, BLOCK), F32),
)
N_REMOTE = 190
N_LOCAL = 16


def main_kernel(queries, passages, dense, entropy, loss, grad_queries, grad_passages, *scratch):
    buf = dict(zip(SCRATCH, scratch))
    send_sems, recv_sems, local_sems = scratch[len(SCRATCH) :]
    qs, ws, tt, lv, st, sr, grid = (buf[k] for k in ("qs", "ws", "tt", "lv", "st", "sr", "grid"))
    go, gs, gr = (buf[k] for k in ("go", "gs", "gr"))
    x, y, z, core = place()
    xh = x // 2
    used = [0, 0]
    sent = []

    def remote(src, dst, target):
        index = used[0]
        used[0] += 1
        copy = pltpu.make_async_remote_copy(
            src_ref=src,
            dst_ref=dst,
            send_sem=send_sems.at[index],
            recv_sem=recv_sems.at[index],
            device_id=target,
            device_id_type=MESH,
        )
        copy.start()
        sent.append(copy)
        return copy

    def local(src, dst):
        index = used[1]
        used[1] += 1
        copy = pltpu.make_async_copy(src, dst, local_sems.at[index])
        copy.start()
        return copy

    sibling = device(x, y, z, 1 - core)
    by_x = {d: device(x + d, y, z, core) for d in (1, 2, 3)}
    by_y = {d: device(x, y + d, z, core) for d in (1, 2, 3)}
    by_z = {d: device(x, y, z + d, core) for d in range(1, NZ)}
    peers = [sibling, *by_x.values(), *by_y.values(), *by_z.values()]

    own_block = local(passages, ws.at[pl.ds(0, SPAN)])
    own_queries = local(queries, qs.at[pl.ds(0, ROWS)])
    own_teacher = local(dense.at[core], tt.at[pl.ds(0, ROWS)])
    barrier = pltpu.get_barrier_semaphore()
    for peer in peers:
        pl.semaphore_signal(barrier, inc=1, device_id=peer, device_id_type=MESH)
    pl.semaphore_wait(barrier, len(peers))

    mine = pl.ds(pl.multiple_of(FLAT + QUARTER * y, LANES), QUARTER)
    flat = pl.ds(0, FLAT)

    def row(dxl, dz):
        return dxl * GROUP + (dz % NZ) * SPAN

    def along_z(dz, way, first=0, count=SPAN):
        target = by_z[1 if way > 0 else NZ - 1]
        here = pl.ds(row(0, dz) + first, count)
        there = pl.ds(row(0, dz - way) + first, count)
        return [remote(ws.at[here, c], ws.at[there, c], target) for c in (mine, flat)]

    def along_x(dz):
        copies = []
        for d, first in ((1, 0), (3, HALF)):
            here = pl.ds(row(0, dz) + first, HALF)
            there = pl.ds(row(1, dz) + first, HALF)
            copies += [remote(ws.at[here, c], ws.at[there, c], by_x[d]) for c in (mine, flat)]
        return copies

    def along_y(dxl, dz):
        here = ws.at[pl.ds(row(dxl, dz), SPAN), mine]
        return [remote(here, here, by_y[d]) for d in (1, 3, 2)]

    def arrived(copies):
        for copy in copies:
            copy.wait_recv()

    own_block.wait()
    x_copies, y_copies = {}, []
    up, down = along_z(0, 1), along_z(0, -1)
    x_copies[0] = along_x(0)
    to_sibling = [
        remote(queries, qs.at[pl.ds(ROWS, ROWS)], sibling),
        remote(dense.at[1 - core], tt.at[pl.ds(ROWS, ROWS)], sibling),
    ]
    for step in (1, 2, 3):
        arrived(up)
        up = along_z(-step, 1, 0, HALF if step == 3 else SPAN)
        x_copies[-step] = along_x(-step)
        y_copies += along_y(0, -step)
        arrived(down)
        if step == 3:
            down = along_z(step, -1, HALF, HALF)
        else:
            down = along_z(step, -1)
        x_copies[step] = along_x(step)
        y_copies += along_y(0, step)
        for dz in {1 - step, step - 1}:
            arrived(x_copies[dz])
            y_copies += along_y(1, dz)
    arrived(up)
    arrived(down)
    x_copies[4] = along_x(4)
    y_copies += along_y(0, 4)
    for dz in (-3, 3, 4):
        arrived(x_copies[dz])
        y_copies += along_y(1, dz)
    own_queries.wait()
    own_teacher.wait()
    arrived(to_sibling)
    arrived(y_copies)

    def dot_rows(a, b):
        return lax.dot_general(a, b, (((1,), (1,)), ((), ())), preferred_element_type=F32)

    column = lax.broadcasted_iota(jnp.int32, (2 * ROWS, W2), 1)
    head = qs[:, 0:W2]
    zero = jnp.zeros_like(head)
    lv[0] = dot_rows(jnp.where(column < W1, head, zero), ws[:, 0:W2])
    lv[1] = lv[0] + dot_rows(jnp.where(column < W1, zero, head), ws[:, 0:W2])
    lv[2] = lv[1] + dot_rows(qs[:, W2:W3], ws[:, W2:W3])
    lv[3] = lv[2]

    def score_step(index, carry):
        cols = pl.ds(pl.multiple_of(index * 1024, 1024), 1024)
        lv[3] += dot_rows(qs[:, cols], ws[:, cols])
        return carry

    lax.fori_loop(1, E // 1024, score_step, 0)

    scales = [1.0 / math.sqrt(width) for width in WIDTHS]
    teacher_or = tt[...]
    chosen = teacher_or >= 0.0
    teacher = jnp.where(chosen, teacher_or, 0.0)
    columns = [None] * 13
    for level in range(4):
        logits = lv[level] * scales[level]
        top = jnp.max(jnp.where(chosen, logits, -BIG), axis=1, keepdims=True)
        shifted = jnp.where(chosen, logits - top, 0.0)
        weight = jnp.where(chosen, jnp.exp(shifted), 0.0)
        lv[level] = weight
        columns[level] = top
        columns[4 + level] = jnp.sum(weight, axis=1, keepdims=True)
        columns[8 + level] = jnp.sum(teacher * shifted, axis=1, keepdims=True)
    columns[12] = jnp.sum(teacher, axis=1, keepdims=True)
    lane = lax.broadcasted_iota(jnp.int32, (2 * ROWS, LANES), 1)
    table = jnp.zeros((2 * ROWS, LANES), F32)
    for index, value in enumerate(columns):
        table = jnp.where(lane == index, value, table)
    st[...] = table
    stats_copy = remote(st, sr, sibling)
    stats_copy.wait_recv()
    received = sr[...]
    other = jnp.concatenate([received[ROWS:], received[:ROWS]], axis=0)
    loss_rows = jnp.zeros((ROWS, 1), F32)
    teacher_sum = (columns[12] + other[:, 12:13])[:ROWS]
    tail = None
    for level in (3, 2, 1, 0):
        top, top_other = columns[level], other[:, level : level + 1]
        peak = jnp.maximum(top, top_other)
        fade, fade_other = jnp.exp(top - peak), jnp.exp(top_other - peak)
        total = columns[4 + level] * fade + other[:, 4 + level : 5 + level] * fade_other
        part = columns[8 + level] + columns[12] * (top - peak)
        part_other = other[:, 8 + level : 9 + level] + other[:, 12:13] * (top_other - peak)
        loss_rows += jnp.log(total[:ROWS]) * teacher_sum - (part + part_other)[:ROWS]
        dlogit = (lv[level] * (fade / total) - teacher) * scales[level]
        tail = dlogit if tail is None else dlogit + tail
        grid[level] = tail.astype(BF16)
    loss[...] = 4.0 * entropy[...] + loss_rows

    pa, pab, pb, pbb, pc, pcb = (buf[k] for k in ("pa", "pab", "pb", "pbb", "pc", "pcb"))

    def dot_columns(a, b):
        return lax.dot_general(a, b, (((0,), (0,)), ((), ())), preferred_element_type=F32)

    def keep(dxl, q, result):
        rounded = result.astype(BF16)
        xh_of, y_of = q // 4, q % 4
        for dz in range(NZ):
            top = slice(dz * SPAN, dz * SPAN + HALF)
            low = slice(dz * SPAN + HALF, (dz + 1) * SPAN)
            whole = slice(dz * SPAN, (dz + 1) * SPAN)
            pa[dz, dxl, q] = result[whole, :WA]
            pab[dz, dxl, q] = rounded[whole, :WA]
            pb[dxl, xh_of, y_of, dz] = result[top, WA:]
            pbb[dxl, xh_of, y_of, dz] = rounded[top, WA:]
            pc[y_of, dxl, xh_of, dz] = result[low, WA:]
            pcb[y_of, dxl, xh_of, dz] = rounded[low, WA:]

    for dxl in range(2):
        part = pl.ds(dxl * GROUP, GROUP)
        narrow = lax.broadcasted_iota(jnp.int32, (GROUP, W2), 1) < W1
        first = qs[:, 0:W2]
        first = jnp.where(
            narrow, dot_columns(grid[0, :, part], first), dot_columns(grid[1, :, part], first)
        )
        second = dot_columns(grid[2, :, part], qs[:, W2:BLOCK])
        keep(dxl, 0, jnp.concatenate([first, second], axis=1))
        keep(dxl, 1, dot_columns(grid[2, :, part], qs[:, BLOCK : 2 * BLOCK]))
        for q in range(2, 8):
            keep(dxl, q, dot_columns(grid[3, :, part], qs[:, q * BLOCK : (q + 1) * BLOCK]))

    ra, rax, ray, fa, ga = (buf[k] for k in ("ra", "rax", "ray", "fa", "ga"))

    def ring(way, step, dxl):
        dz = (way * (5 - step)) % NZ
        target = by_z[1 if way > 0 else NZ - 1]
        slot = ra.at[0 if way > 0 else 1, step - 1, dxl]
        if step == 1:
            rows = pl.ds(0 if way > 0 else HALF, HALF)
            return remote(pab.at[dz, dxl, :, rows], slot.at[:, rows], target)
        return remote(pab.at[dz, dxl], slot, target)

    def toward(d):
        return ((x + d) % NX) // 2

    rings = {(way, dxl): ring(way, 1, dxl) for dxl in range(2) for way in (1, -1)}
    b_copies = [remote(pbb.at[d % 2, toward(d)], buf["rbx"].at[d - 1], by_x[d]) for d in (1, 2, 3)]
    c_copies = [remote(pcb.at[(y + d) % NY], buf["rcy"].at[d - 1], by_y[d]) for d in (1, 2, 3)]

    def dot_plain(a, b):
        return jnp.dot(a, b, preferred_element_type=F32)

    def keep_query(cols, result):
        go[:, cols] = result[:ROWS]
        gs[:, cols] = result[ROWS:]

    first = ws[:, 0:W2]
    keep_query(
        slice(0, W2), jnp.where(column < W1, dot_plain(grid[0], first), dot_plain(grid[1], first))
    )
    keep_query(slice(W2, BLOCK), dot_plain(grid[2], ws[:, W2:BLOCK]))
    keep_query(slice(BLOCK, W3), dot_plain(grid[2], ws[:, BLOCK:W3]))

    def query_step(index, carry):
        cols = pl.ds(pl.multiple_of(index * BLOCK, BLOCK), BLOCK)
        keep_query(cols, dot_plain(grid[3], ws[:, cols]))
        return carry

    lax.fori_loop(2, E // BLOCK, query_step, 0)
    query_copy = remote(gs, gr, sibling)

    for step in (1, 2, 3):
        for dxl in range(2):
            for way in (1, -1):
                rings[way, dxl].wait_recv()
                dz = (way * (4 - step)) % NZ
                slot = ra.at[0 if way > 0 else 1, step - 1, dxl]
                rows = pl.ds(0, SPAN)
                if step == 1:
                    rows = pl.ds(0 if way > 0 else HALF, HALF)
                pab[dz, dxl, :, rows] = (pa[dz, dxl, :, rows] + slot[:, rows].astype(F32)).astype(
                    BF16
                )
                rings[way, dxl] = ring(way, step + 1, dxl)
        if step == 1:
            query_copy.wait_recv()
            go[...] += gr[...]
            out_copy = local(go, grad_queries)
    for dxl in range(2):
        rings[1, dxl].wait_recv()
        rings[-1, dxl].wait_recv()
        total = pa[0, dxl] + ra[0, 3, dxl].astype(F32) + ra[1, 3, dxl].astype(F32)
        fa[dxl] = total.reshape(2, 4, SPAN, WA)
    ax_copies = [remote(fa.at[d % 2, toward(d)], rax.at[d - 1], by_x[d]) for d in (1, 2, 3)]

    gb, gbb, rbx, rby, hb, rbz = (buf[k] for k in ("gb", "gbb", "rbx", "rby", "hb", "rbz"))
    gc, gcb, rcy, rcx, hc, rcz = (buf[k] for k in ("gc", "gcb", "rcy", "rcx", "hc", "rcz"))
    arrived(b_copies)
    total = pb[0, xh] + rbx[0].astype(F32) + rbx[1].astype(F32) + rbx[2].astype(F32)
    gb[...] = total
    gbb[...] = total.astype(BF16)
    b_copies = [remote(gbb.at[(y + d) % NY], rby.at[d - 1], by_y[d]) for d in (1, 2, 3)]
    arrived(c_copies)
    total = pc[y] + rcy[0].astype(F32) + rcy[1].astype(F32) + rcy[2].astype(F32)
    gc[...] = total
    gcb[...] = total.astype(BF16)
    c_copies = [remote(gcb.at[d % 2, toward(d)], rcx.at[d - 1], by_x[d]) for d in (1, 2, 3)]
    arrived(ax_copies)
    ga[...] = fa[0, xh] + rax[0] + rax[1] + rax[2]
    ay_copies = [remote(ga.at[(y + d) % NY], ray.at[d - 1], by_y[d]) for d in (1, 2, 3)]

    arrived(b_copies)
    hb[...] = gb[y] + rby[0].astype(F32) + rby[1].astype(F32) + rby[2].astype(F32)
    bz_copies = [remote(hb.at[d], rbz.at[d - 1], by_z[d]) for d in range(1, NZ)]
    arrived(c_copies)
    hc[...] = gc[0, xh] + rcx[0].astype(F32) + rcx[1].astype(F32) + rcx[2].astype(F32)
    cz_copies = [remote(hc.at[d], rcz.at[d - 1], by_z[d]) for d in range(1, NZ)]
    arrived(ay_copies)
    ob = buf["ob"]
    ob[:, :WA] = ga[y] + ray[0] + ray[1] + ray[2]
    arrived(bz_copies)
    arrived(cz_copies)
    total_b, total_c = hb[0], hc[0]
    for index in range(NZ - 1):
        total_b += rbz[index]
        total_c += rcz[index]
    ob[:HALF, WA:] = total_b
    ob[HALF:, WA:] = total_c
    last = local(ob, grad_passages)
    for copy in sent:
        copy.wait_send()
    out_copy.wait()
    last.wait()


def main_call(queries, passages, dense, entropy):
    scratch = [pltpu.VMEM(shape, dtype) for shape, dtype in SCRATCH.values()]
    scratch += [
        pltpu.SemaphoreType.DMA((N_REMOTE,)),
        pltpu.SemaphoreType.DMA((N_REMOTE,)),
        pltpu.SemaphoreType.DMA((N_LOCAL,)),
    ]
    anywhere = pl.BlockSpec(memory_space=pl.ANY)
    return pl.pallas_call(
        main_kernel,
        out_shape=(
            jax.ShapeDtypeStruct((ROWS, LANES), F32),
            jax.ShapeDtypeStruct((ROWS, E), F32),
            jax.ShapeDtypeStruct((SPAN, BLOCK), F32),
        ),
        in_specs=[anywhere, anywhere, anywhere, pl.BlockSpec(memory_space=pltpu.VMEM)],
        out_specs=(pl.BlockSpec(memory_space=pltpu.VMEM), anywhere, anywhere),
        scratch_shapes=scratch,
        compiler_params=pltpu.CompilerParams(
            collective_id=0, has_side_effects=True, vmem_limit_bytes=60 * 2**20
        ),
        name="distill",
    )(queries, passages, dense, entropy)


def shards(queries, passages, candidates, teacher_scores):
    dense, entropy = prepare(candidates, teacher_scores)
    loss, grad_queries, grad_passages = main_call(queries, passages, dense, entropy)
    return (loss[:, 0], grad_queries, grad_passages)


def solution(mesh):
    return jax.shard_map(
        shards,
        mesh=mesh,
        in_specs=(
            P(("query", "passage"), None),
            P("passage", None),
            P(("query", "passage"), None),
            P(("query", "passage"), None),
        ),
        out_specs=(P(("query", "passage")), P(("query", "passage"), None), P("passage", "query")),
        check_vma=False,
    )
```

```python
import functools
import math

import jax
import jax.numpy as jnp
from jax import lax
from jax.experimental import pallas as pl
from jax.experimental.pallas import tpu as pltpu
from jax.sharding import PartitionSpec as P

MESH = pl.DeviceIdType.MESH
BF16 = jnp.bfloat16
F32 = jnp.float32

E = 4096
W1, W2, W3 = 64, 256, 1024
WIDTHS = (W1, W2, W3, E)
ROWS = 128
SPAN = 32
HALF = 16
NX, NY, NZ = 4, 4, 8
POOL = 2 * NZ * SPAN
GROUP = NZ * SPAN
LANES = 128
BIG = 3.0e38

QUARTER = 384
FLAT = E - 4 * QUARTER
PIECES = 2
GATHER_ORDER = (
    ('m', 1), ('x', 0), (0, 1), (1, 1), ('m', 2), ('x', 1), (0, 2), (1, 2), ('m', 3), ('x', 2), (0, 3), (1, 3), ('m', 4), ('x', 3), (0, 4), (1, 4), ('x', 4)
)

BLOCK = 512
WA = 128
WB = BLOCK - WA
FIRST_Z = 2
CHUNKS = ((0, 5), (5, 3))


def place():
    query = lax.axis_index("query")
    passage = lax.axis_index("passage")
    x = (query // 4) * 2 + (passage // 2) % 2
    return x, query % 4, passage // 4, passage % 2


def device(x, y, z, core):
    x, y, z = x % NX, y % NY, z % NZ
    return ((x // 2) * 4 + y, (z * 2 + x % 2) * 2 + core)


SCRATCH = dict(
    qs=((2 * ROWS, E), BF16),
    ws=((2 * GROUP, E), BF16),
    cs=((2 * ROWS, LANES), jnp.int32),
    rs=((2 * ROWS, LANES), F32),
    ts=((2 * ROWS, LANES), F32),
    tt=((2 * ROWS, POOL), F32),
    lv=((4, 2 * ROWS, POOL), F32),
    st=((2 * ROWS, LANES), F32),
    sr=((2 * ROWS, LANES), F32),
    grid=((4, 2 * ROWS, POOL), BF16),
    go=((ROWS, E), F32),
    gs=((ROWS, E), F32),
    gr=((ROWS, E), F32),
    pa=((NZ, 2, 8, SPAN, WA), F32),
    pab=((NZ, 2, 8, SPAN, WA), BF16),
    ra=((2, 4, 2, 8, SPAN, WA), BF16),
    fa=((2, 2, 4, SPAN, WA), F32),
    rax=((3, 4, SPAN, WA), F32),
    ga=((4, SPAN, WA), F32),
    ray=((3, SPAN, WA), F32),
    pb=((2, 2, 4, NZ, HALF, WB), F32),
    pbb=((2, 2, 4, NZ, HALF, WB), BF16),
    rbx=((3, 4, NZ, HALF, WB), BF16),
    gb=((4, NZ, HALF, WB), F32),
    gbb=((4, NZ, HALF, WB), BF16),
    rby=((3, NZ, HALF, WB), BF16),
    hb=((NZ, HALF, WB), F32),
    hbb=((NZ, HALF, WB), BF16),
    rbz=((NZ, HALF, WB), F32),
    rbzb=((NZ, HALF, WB), BF16),
    pc=((4, 2, 2, NZ, HALF, WB), F32),
    pcb=((4, 2, 2, NZ, HALF, WB), BF16),
    rcy=((3, 2, 2, NZ, HALF, WB), BF16),
    gc=((2, 2, NZ, HALF, WB), F32),
    gcb=((2, 2, NZ, HALF, WB), BF16),
    rcx=((3, NZ, HALF, WB), BF16),
    hc=((NZ, HALF, WB), F32),
    hcb=((NZ, HALF, WB), BF16),
    rcz=((NZ, HALF, WB), F32),
    rczb=((NZ, HALF, WB), BF16),
    ob=((SPAN, BLOCK), F32),
)
N_REMOTE = 260
N_LOCAL = 16


def main_kernel(queries, passages, candidates, scores, loss, grad_queries, grad_passages, *scratch):
    buf = dict(zip(SCRATCH, scratch))
    send_sems, recv_sems, local_sems = scratch[len(SCRATCH) :]
    qs, ws, tt, lv, st, sr, grid = (buf[k] for k in ("qs", "ws", "tt", "lv", "st", "sr", "grid"))
    go, gs, gr = (buf[k] for k in ("go", "gs", "gr"))
    x, y, z, core = place()
    xh = x // 2
    used = [0, 0]
    sent = []

    def remote(src, dst, target):
        index = used[0]
        used[0] += 1
        copy = pltpu.make_async_remote_copy(
            src_ref=src,
            dst_ref=dst,
            send_sem=send_sems.at[index],
            recv_sem=recv_sems.at[index],
            device_id=target,
            device_id_type=MESH,
        )
        copy.start()
        sent.append(copy)
        return copy

    def local(src, dst):
        index = used[1]
        used[1] += 1
        copy = pltpu.make_async_copy(src, dst, local_sems.at[index])
        copy.start()
        return copy

    sibling = device(x, y, z, 1 - core)
    by_x = {d: device(x + d, y, z, core) for d in (1, 2, 3)}
    by_y = {d: device(x, y + d, z, core) for d in (1, 2, 3)}
    by_z = {d: device(x, y, z + d, core) for d in range(1, NZ)}
    peers = [sibling, *by_x.values(), *by_y.values(), *by_z.values()]

    own_block = local(passages, ws.at[pl.ds(0, SPAN)])
    own_queries = local(queries, qs.at[pl.ds(0, ROWS)])
    own_teacher = [
        local(candidates, buf["cs"].at[pl.ds(0, ROWS)]),
        local(scores, buf["rs"].at[pl.ds(0, ROWS)]),
    ]
    barrier = pltpu.get_barrier_semaphore()
    for peer in peers:
        pl.semaphore_signal(barrier, inc=1, device_id=peer, device_id_type=MESH)
    pl.semaphore_wait(barrier, len(peers))

    mine = pl.ds(pl.multiple_of(FLAT + QUARTER * y, LANES), QUARTER)
    pieces = {"m": mine}
    for index in range(PIECES):
        pieces[index] = pl.ds(index * (FLAT // PIECES), FLAT // PIECES)

    def row(dxl, dz):
        return dxl * GROUP + (dz % NZ) * SPAN

    z_copies, x_copies, y_copies = {}, {}, ([], [])

    def along_z(piece, step, way):
        dz, cols = -way * step, pieces[piece]
        first, count = (0 if way > 0 else HALF, HALF) if step == 3 else (0, SPAN)
        here = pl.ds(row(0, dz) + first, count)
        there = pl.ds(row(0, dz - way) + first, count)
        target = by_z[1 if way > 0 else NZ - 1]
        z_copies[piece, step + 1, way] = remote(ws.at[here, cols], ws.at[there, cols], target)

    def along_x(piece, dz):
        cols = pieces[piece]
        copies = []
        for d, first in ((1, 0), (3, HALF)):
            here = pl.ds(row(0, dz) + first, HALF)
            there = pl.ds(row(1, dz) + first, HALF)
            copies.append(remote(ws.at[here, cols], ws.at[there, cols], by_x[d]))
        x_copies[piece, dz] = copies

    def along_y(dxl, dz):
        here = ws.at[pl.ds(row(dxl, dz), SPAN), mine]
        for d in (1, 3, 2):
            y_copies[dxl].append(remote(here, here, by_y[d]))

    def arrived_here(copies):
        for copy in copies:
            copy.wait()

    def arrived(copies):
        for copy in copies:
            copy.wait_recv()

    own_block.wait()
    for piece in ('m', 0, 1):
        for way in (1, -1):
            along_z(piece, 0, way)
        along_x(piece, 0)
    to_sibling = [
        remote(candidates, buf["cs"].at[pl.ds(ROWS, ROWS)], sibling),
        remote(scores, buf["rs"].at[pl.ds(ROWS, ROWS)], sibling),
        remote(queries, qs.at[pl.ds(ROWS, ROWS)], sibling),
    ]
    x_done = set()

    def from_x(piece, dz):
        arrived(x_copies[piece, dz])
        x_done.add((piece, dz))
        if piece == "m":
            along_y(1, dz)

    cs, rs, ts = buf["cs"], buf["rs"], buf["ts"]
    lane = lax.broadcasted_iota(jnp.int32, (ROWS, LANES), 1)
    entropy = []

    def teach(rows):
        raw = rs[rows]
        shifted = raw - jnp.max(raw, axis=1, keepdims=True)
        log_teacher = shifted - jnp.log(jnp.sum(jnp.exp(shifted), axis=1, keepdims=True))
        value = jnp.exp(log_teacher)
        ts[rows] = value
        entropy.append(jnp.sum(value * log_teacher, axis=1, keepdims=True))

    def spread(rows, chunk):
        chosen = cs[rows]
        slot = lane // SPAN + chunk * (LANES // SPAN)
        dxl, dz = slot // NZ, slot % NZ
        owner = (((z + dz) % NZ) * 2 + (x + dxl) % 2) * 2 + core
        target = owner * SPAN + lane % SPAN
        position = jnp.zeros((ROWS, LANES), jnp.int32)
        for step in (64, 32, 16, 8, 4, 2, 1):
            probe = jnp.take_along_axis(chosen, position + (step - 1), axis=1)
            position = jnp.where(probe < target, position + step, position)
        hit = jnp.take_along_axis(chosen, position, axis=1) == target
        value = jnp.take_along_axis(ts[rows], position, axis=1)
        tt[rows, chunk * LANES : (chunk + 1) * LANES] = jnp.where(hit, value, -1.0)

    own, other = pl.ds(0, ROWS), pl.ds(ROWS, ROWS)
    chores = [lambda: (arrived_here(own_teacher), teach(own))]
    chores += [lambda chunk=chunk: spread(own, chunk) for chunk in range(POOL // LANES)]
    chores += [lambda: (arrived(to_sibling[:2]), teach(other))]
    chores += [lambda chunk=chunk: spread(other, chunk) for chunk in range(POOL // LANES)]

    for piece, step in GATHER_ORDER:
        if piece == "x":
            for dz in ((0,) if step == 0 else (4,) if step == 4 else (-step, step)):
                from_x("m", dz)
            continue
        for way in (1, -1):
            z_copies[piece, step, way].wait_recv()
            if step < 4:
                along_z(piece, step, way)
                along_x(piece, -way * step)
                if piece == "m":
                    along_y(0, -way * step)
        if step == 4:
            along_x(piece, 4)
            if piece == "m":
                along_y(0, 4)
        if chores and (piece, step) != ("m", 1):
            chores.pop(0)()
    for chore in chores:
        chore()
    def dot_rows(a, b):
        return lax.dot_general(a, b, (((1,), (1,)), ((), ())), preferred_element_type=F32)

    column = lax.broadcasted_iota(jnp.int32, (2 * ROWS, W2), 1)
    own_queries.wait()
    arrived(to_sibling[2:])
    for dxl in range(2):
        if dxl == 1:
            for key in x_copies:
                if key not in x_done:
                    from_x(*key)
        arrived(y_copies[dxl])
        if dxl == 1:
            pass
        rows = pl.ds(dxl * GROUP, GROUP)
        head = qs[:, 0:W2]
        zero = jnp.zeros_like(head)
        narrow = ws[rows, 0:W2]
        level = dot_rows(jnp.where(column < W1, head, zero), narrow)
        lv[0, :, rows] = level
        level += dot_rows(jnp.where(column < W1, zero, head), narrow)
        lv[1, :, rows] = level
        level += dot_rows(qs[:, W2:W3], ws[rows, W2:W3])
        lv[2, :, rows] = level

        def score_step(index, total, rows=rows):
            cols = pl.ds(pl.multiple_of(index * 1024, 1024), 1024)
            return total + dot_rows(qs[:, cols], ws[rows, cols])

        lv[3, :, rows] = lax.fori_loop(1, E // 1024, score_step, level)


    scales = [1.0 / math.sqrt(width) for width in WIDTHS]
    teacher_or = tt[...]
    chosen = teacher_or >= 0.0
    teacher = jnp.where(chosen, teacher_or, 0.0)
    columns = [None] * 13
    for level in range(4):
        logits = lv[level] * scales[level]
        top = jnp.max(jnp.where(chosen, logits, -BIG), axis=1, keepdims=True)
        shifted = jnp.where(chosen, logits - top, 0.0)
        weight = jnp.where(chosen, jnp.exp(shifted), 0.0)
        lv[level] = weight
        columns[level] = top
        columns[4 + level] = jnp.sum(weight, axis=1, keepdims=True)
        columns[8 + level] = jnp.sum(teacher * shifted, axis=1, keepdims=True)
    columns[12] = jnp.sum(teacher, axis=1, keepdims=True)
    place_of = lax.broadcasted_iota(jnp.int32, (2 * ROWS, LANES), 1)
    table = jnp.zeros((2 * ROWS, LANES), F32)
    for index, value in enumerate(columns):
        table = jnp.where(place_of == index, value, table)
    st[...] = table
    stats_copy = remote(st, sr, sibling)
    stats_copy.wait_recv()
    received = sr[...]
    swapped = jnp.concatenate([received[ROWS:], received[:ROWS]], axis=0)
    loss_rows = jnp.zeros((ROWS, 1), F32)
    teacher_sum = (columns[12] + swapped[:, 12:13])[:ROWS]
    tail = None
    for level in (3, 2, 1, 0):
        top, top_other = columns[level], swapped[:, level : level + 1]
        peak = jnp.maximum(top, top_other)
        fade, fade_other = jnp.exp(top - peak), jnp.exp(top_other - peak)
        total = columns[4 + level] * fade + swapped[:, 4 + level : 5 + level] * fade_other
        part = columns[8 + level] + columns[12] * (top - peak)
        part_other = swapped[:, 8 + level : 9 + level] + swapped[:, 12:13] * (top_other - peak)
        loss_rows += jnp.log(total[:ROWS]) * teacher_sum - (part + part_other)[:ROWS]
        dlogit = (lv[level] * (fade / total) - teacher) * scales[level]
        tail = dlogit if tail is None else dlogit + tail
        grid[level] = tail.astype(BF16)
    diagonal = lax.broadcasted_iota(jnp.int32, (ROWS, LANES), 0) == lax.broadcasted_iota(
        jnp.int32, (ROWS, LANES), 1
    )
    loss_rows += 4.0 * entropy[0]
    loss[...] = jnp.sum(jnp.where(diagonal, loss_rows, 0.0), axis=0, keepdims=True)


    pa, pab, pb, pbb, pc, pcb = (buf[k] for k in ("pa", "pab", "pb", "pbb", "pc", "pcb"))

    def dot_columns(a, b):
        return lax.dot_general(a, b, (((0,), (0,)), ((), ())), preferred_element_type=F32)

    def keep(dxl, q, result):
        rounded = result.astype(BF16)
        xh_of, y_of = q // 4, q % 4
        for dz in range(NZ):
            top = slice(dz * SPAN, dz * SPAN + HALF)
            low = slice(dz * SPAN + HALF, (dz + 1) * SPAN)
            whole = slice(dz * SPAN, (dz + 1) * SPAN)
            pa[dz, dxl, q] = result[whole, :WA]
            pab[dz, dxl, q] = rounded[whole, :WA]
            at = (dz - FIRST_Z) % NZ
            pb[dxl, xh_of, y_of, at] = result[top, WA:]
            pbb[dxl, xh_of, y_of, at] = rounded[top, WA:]
            pc[y_of, dxl, xh_of, at] = result[low, WA:]
            pcb[y_of, dxl, xh_of, at] = rounded[low, WA:]

    for dxl in range(2):
        part = pl.ds(dxl * GROUP, GROUP)
        narrow = lax.broadcasted_iota(jnp.int32, (GROUP, W2), 1) < W1
        first = qs[:, 0:W2]
        first = jnp.where(
            narrow, dot_columns(grid[0, :, part], first), dot_columns(grid[1, :, part], first)
        )
        second = dot_columns(grid[2, :, part], qs[:, W2:BLOCK])
        keep(dxl, 0, jnp.concatenate([first, second], axis=1))
        keep(dxl, 1, dot_columns(grid[2, :, part], qs[:, BLOCK : 2 * BLOCK]))
        for q in range(2, 8):
            keep(dxl, q, dot_columns(grid[3, :, part], qs[:, q * BLOCK : (q + 1) * BLOCK]))


    ra, rax, ray, fa, ga = (buf[k] for k in ("ra", "rax", "ray", "fa", "ga"))

    def ring(way, step, dxl):
        dz = (way * (5 - step)) % NZ
        target = by_z[1 if way > 0 else NZ - 1]
        slot = ra.at[0 if way > 0 else 1, step - 1, dxl]
        if step == 1:
            rows = pl.ds(0 if way > 0 else HALF, HALF)
            return remote(pab.at[dz, dxl, :, rows], slot.at[:, rows], target)
        return remote(pab.at[dz, dxl], slot, target)

    def toward(d):
        return ((x + d) % NX) // 2

    rings = {(way, dxl): ring(way, 1, dxl) for dxl in range(2) for way in (1, -1)}
    gb, gbb, rbx, rby = (buf[k] for k in ("gb", "gbb", "rbx", "rby"))
    gc, gcb, rcy, rcx = (buf[k] for k in ("gc", "gcb", "rcy", "rcx"))
    b_copies, c_copies = [], []
    for start, count in CHUNKS:
        part = pl.ds(start, count)
        b_copies.append(
            [
                remote(pbb.at[d % 2, toward(d), :, part], rbx.at[d - 1, :, part], by_x[d])
                for d in (2, 1, 3)
            ]
        )
        c_copies.append(
            [
                remote(pcb.at[(y + d) % NY, :, :, part], rcy.at[d - 1, :, :, part], by_y[d])
                for d in (2, 1, 3)
            ]
        )

    def dot_plain(a, b):
        return jnp.dot(a, b, preferred_element_type=F32)

    def keep_query(cols, result):
        go[:, cols] = result[:ROWS]
        gs[:, cols] = result[ROWS:]

    first = ws[:, 0:W2]
    keep_query(
        slice(0, W2), jnp.where(column < W1, dot_plain(grid[0], first), dot_plain(grid[1], first))
    )
    keep_query(slice(W2, BLOCK), dot_plain(grid[2], ws[:, W2:BLOCK]))
    keep_query(slice(BLOCK, W3), dot_plain(grid[2], ws[:, BLOCK:W3]))

    def query_step(index, carry):
        cols = pl.ds(pl.multiple_of(index * BLOCK, BLOCK), BLOCK)
        keep_query(cols, dot_plain(grid[3], ws[:, cols]))
        return carry

    lax.fori_loop(2, E // BLOCK, query_step, 0)
    query_copy = remote(gs, gr, sibling)

    def ring_step(step):
        for dxl in range(2):
            for way in (1, -1):
                rings[way, dxl].wait_recv()
                dz = (way * (4 - step)) % NZ
                slot = ra.at[0 if way > 0 else 1, step - 1, dxl]
                rows = pl.ds(0, SPAN)
                if step == 1:
                    rows = pl.ds(0 if way > 0 else HALF, HALF)
                pab[dz, dxl, :, rows] = (pa[dz, dxl, :, rows] + slot[:, rows].astype(F32)).astype(
                    BF16
                )
                rings[way, dxl] = ring(way, step + 1, dxl)

    def ring_end():
        for dxl in range(2):
            rings[1, dxl].wait_recv()
            rings[-1, dxl].wait_recv()
            total = pa[0, dxl] + ra[0, 3, dxl].astype(F32) + ra[1, 3, dxl].astype(F32)
            fa[dxl] = total.reshape(2, 4, SPAN, WA)
        return [remote(fa.at[d % 2, toward(d)], rax.at[d - 1], by_x[d]) for d in (1, 2, 3)]

    def three(own, parts):
        return own + parts[0].astype(F32) + parts[1].astype(F32) + parts[2].astype(F32)

    def b_second(chunk):
        part = pl.ds(*CHUNKS[chunk])
        arrived(b_copies[chunk])
        total = three(pb[0, xh, :, part], rbx[:, :, part])
        gb[:, part] = total
        gbb[:, part] = total.astype(BF16)
        return [
            remote(gbb.at[(y + d) % NY, part], rby.at[d - 1, part], by_y[d]) for d in (2, 1, 3)
        ]

    def c_second(chunk):
        part = pl.ds(*CHUNKS[chunk])
        arrived(c_copies[chunk])
        total = three(pc[y, :, :, part], rcy[:, :, :, part])
        gc[:, :, part] = total
        gcb[:, :, part] = total.astype(BF16)
        return [
            remote(gcb.at[d % 2, toward(d), part], rcx.at[d - 1, part], by_x[d]) for d in (2, 1, 3)
        ]

    def third(chunk, total, wide, narrow, wide_in, narrow_in):
        start, count = CHUNKS[chunk]
        wide[pl.ds(start, count)] = total
        narrow[pl.ds(start, count)] = total.astype(BF16)
        copies = []
        for at in range(start, start + count):
            dz = (at + FIRST_Z) % NZ
            if dz and chunk == 0:
                copies.append(remote(narrow.at[at], narrow_in.at[at], by_z[dz]))
            elif dz:
                copies.append(remote(wide.at[at], wide_in.at[at], by_z[dz]))
        return copies

    hb, hbb, rbz, rbzb = (buf[k] for k in ("hb", "hbb", "rbz", "rbzb"))
    hc, hcb, rcz, rczb = (buf[k] for k in ("hc", "hcb", "rcz", "rczb"))

    def b_third(chunk):
        part = pl.ds(*CHUNKS[chunk])
        arrived(b_next[chunk])
        return third(chunk, three(gb[y, part], rby[:, part]), hb, hbb, rbz, rbzb)

    def c_third(chunk):
        part = pl.ds(*CHUNKS[chunk])
        arrived(c_next[chunk])
        return third(chunk, three(gc[0, xh, part], rcx[:, part]), hc, hcb, rcz, rczb)

    ring_step(1)
    ring_step(2)
    query_copy.wait_recv()
    go[...] += gr[...]
    out_copy = local(go, grad_queries)
    ring_step(3)
    b_next, c_next, last_copies = [None, None], [None, None], []
    b_next[0] = b_second(0)
    c_next[0] = c_second(0)
    ax_copies = ring_end()
    last_copies += b_third(0)
    last_copies += c_third(0)
    b_next[1] = b_second(1)
    c_next[1] = c_second(1)
    arrived(ax_copies)
    ga[...] = three(fa[0, xh], rax)
    ay_copies = [remote(ga.at[(y + d) % NY], ray.at[d - 1], by_y[d]) for d in (1, 2, 3)]
    last_copies += b_third(1)
    last_copies += c_third(1)
    arrived(ay_copies)
    ob = buf["ob"]
    ob[:, :WA] = three(ga[y], ray)
    arrived(last_copies)
    at_home = (0 - FIRST_Z) % NZ
    total_b, total_c = hb[at_home], hc[at_home]
    for at in range(NZ):
        if at < CHUNKS[0][1]:
            total_b += rbzb[at].astype(F32)
            total_c += rczb[at].astype(F32)
        elif at != at_home:
            total_b += rbz[at]
            total_c += rcz[at]
    ob[:HALF, WA:] = total_b
    ob[HALF:, WA:] = total_c
    last = local(ob, grad_passages)
    for copy in sent:
        copy.wait_send()
    out_copy.wait()
    last.wait()


def main_call(queries, passages, candidates, scores):
    scratch = [pltpu.VMEM(shape, dtype) for shape, dtype in SCRATCH.values()]
    scratch += [
        pltpu.SemaphoreType.DMA((N_REMOTE,)),
        pltpu.SemaphoreType.DMA((N_REMOTE,)),
        pltpu.SemaphoreType.DMA((N_LOCAL,)),
    ]
    anywhere = pl.BlockSpec(memory_space=pl.ANY)
    return pl.pallas_call(
        main_kernel,
        out_shape=(
            jax.ShapeDtypeStruct((1, ROWS), F32),
            jax.ShapeDtypeStruct((ROWS, E), F32),
            jax.ShapeDtypeStruct((SPAN, BLOCK), F32),
        ),
        in_specs=[anywhere] * 4,
        out_specs=(pl.BlockSpec(memory_space=pltpu.VMEM), anywhere, anywhere),
        scratch_shapes=scratch,
        compiler_params=pltpu.CompilerParams(
            collective_id=0, has_side_effects=True, vmem_limit_bytes=60 * 2**20
        ),
        name="distill",
    )(queries, passages, candidates, scores)


def shards(queries, passages, candidates, teacher_scores):
    loss, grad_queries, grad_passages = main_call(queries, passages, candidates, teacher_scores)
    return (loss.reshape(ROWS), grad_queries, grad_passages)


def solution(mesh):
    return jax.shard_map(
        shards,
        mesh=mesh,
        in_specs=(
            P(("query", "passage"), None),
            P("passage", None),
            P(("query", "passage"), None),
            P(("query", "passage"), None),
        ),
        out_specs=(P(("query", "passage")), P(("query", "passage"), None), P("passage", "query")),
        check_vma=False,
    )
```

```python
import functools
import math

import jax
import jax.numpy as jnp
from jax import lax
from jax.experimental import pallas as pl
from jax.experimental.pallas import tpu as pltpu
from jax.sharding import PartitionSpec as P

MESH = pl.DeviceIdType.MESH
BF16 = jnp.bfloat16
F32 = jnp.float32

E = 4096
W1, W2, W3 = 64, 256, 1024
WIDTHS = (W1, W2, W3, E)
ROWS = 128
SPAN = 32
HALF = 16
NX, NY, NZ = 4, 4, 8
POOL = 2 * NZ * SPAN
GROUP = NZ * SPAN
LANES = 128
BIG = 3.0e38
PIECE = 16
STRIP = 32

QUARTER = 384
FLAT = E - 4 * QUARTER
PIECES = 2
GATHER_ORDER = (
    ('m', 1), ('x', 0), (0, 1), (1, 1), ('m', 2), ('x', 1), (0, 2), (1, 2), ('m', 3), ('x', 2), (0, 3), (1, 3), ('m', 4), ('x', 3), (0, 4), (1, 4), ('x', 4)
)

BLOCK = 512
WA = 128
WB = BLOCK - WA
FIRST_Z = 2
CHUNKS = ((0, 5), (5, 3))
FAR = (3, 4, 5)


def place():
    query = lax.axis_index("query")
    passage = lax.axis_index("passage")
    x = (query // 4) * 2 + (passage // 2) % 2
    return x, query % 4, passage // 4, passage % 2


def device(x, y, z, core):
    x, y, z = x % NX, y % NY, z % NZ
    return ((x // 2) * 4 + y, (z * 2 + x % 2) * 2 + core)


SCRATCH = dict(
    qs=((2 * ROWS, E), BF16),
    ws=((2 * GROUP, E), BF16),
    cs=((2 * ROWS, LANES), jnp.int32),
    rs=((2 * ROWS, LANES), F32),
    ts=((2 * ROWS, LANES), F32),
    tt=((2 * ROWS, POOL), F32),
    lv=((4, 2 * ROWS, POOL), F32),
    st=((3, 2 * ROWS, LANES), F32),
    sr=((3, 2 * ROWS, LANES), F32),
    grid=((4, 2 * ROWS, POOL), BF16),
    go=((ROWS, E), F32),
    gs=((ROWS, E), F32),
    gr=((ROWS, E), F32),
    pa=((NZ, 2, 8, SPAN, WA), F32),
    pab=((NZ, 2, 8, SPAN, WA), BF16),
    ra=((2, 4, 2, 8, SPAN, WA), BF16),
    fa=((2, 2, 4, SPAN, WA), F32),
    rax=((3, 4, SPAN, WA), F32),
    ga=((4, SPAN, WA), F32),
    ray=((3, SPAN, WA), F32),
    pb=((2, 2, 4, NZ, HALF, WB), F32),
    pbb=((2, 2, 4, NZ, HALF, WB), BF16),
    rbr=((2, 2, NZ, HALF, WB), BF16),
    rbx=((2, 4, NZ, HALF, WB), BF16),
    gb=((4, NZ, HALF, WB), F32),
    gbb=((4, NZ, HALF, WB), BF16),
    rby=((3, NZ, HALF, WB), BF16),
    hb=((NZ, HALF, WB), F32),
    hbb=((NZ, HALF, WB), BF16),
    rbz=((NZ, HALF, WB), F32),
    rbzb=((NZ, HALF, WB), BF16),
    pc=((4, 2, 2, NZ, HALF, WB), F32),
    pcb=((4, 2, 2, NZ, HALF, WB), BF16),
    rcr=((2, 2, NZ, HALF, WB), BF16),
    rcy=((2, 2, 2, NZ, HALF, WB), BF16),
    gc=((2, 2, NZ, HALF, WB), F32),
    gcb=((2, 2, NZ, HALF, WB), BF16),
    rcx=((3, NZ, HALF, WB), BF16),
    hc=((NZ, HALF, WB), F32),
    hcb=((NZ, HALF, WB), BF16),
    rcz=((NZ, HALF, WB), F32),
    rczb=((NZ, HALF, WB), BF16),
    ob=((SPAN, BLOCK), F32),
)
N_REMOTE = 260
N_LOCAL = 16


def main_kernel(queries, passages, candidates, scores, loss, grad_queries, grad_passages, *scratch):
    buf = dict(zip(SCRATCH, scratch))
    send_sems, recv_sems, local_sems = scratch[len(SCRATCH) :]
    qs, ws, tt, lv, st, sr, grid = (buf[k] for k in ("qs", "ws", "tt", "lv", "st", "sr", "grid"))
    go, gs, gr = (buf[k] for k in ("go", "gs", "gr"))
    x, y, z, core = place()
    xh = x // 2
    used = [0, 0]
    sent = []

    def remote(src, dst, target):
        index = used[0]
        used[0] += 1
        copy = pltpu.make_async_remote_copy(
            src_ref=src,
            dst_ref=dst,
            send_sem=send_sems.at[index],
            recv_sem=recv_sems.at[index],
            device_id=target,
            device_id_type=MESH,
        )
        copy.start()
        sent.append(copy)
        return copy

    def local(src, dst):
        index = used[1]
        used[1] += 1
        copy = pltpu.make_async_copy(src, dst, local_sems.at[index])
        copy.start()
        return copy

    sibling = device(x, y, z, 1 - core)
    by_x = {d: device(x + d, y, z, core) for d in (1, 2, 3)}
    by_y = {d: device(x, y + d, z, core) for d in (1, 2, 3)}
    by_z = {d: device(x, y, z + d, core) for d in range(1, NZ)}
    peers = [sibling, *by_x.values(), *by_y.values(), by_z[1], by_z[NZ - 1]]

    own_block = local(passages, ws.at[pl.ds(0, SPAN)])
    own_queries = local(queries, qs.at[pl.ds(0, ROWS)])
    own_teacher = [
        local(candidates, buf["cs"].at[pl.ds(0, ROWS)]),
        local(scores, buf["rs"].at[pl.ds(0, ROWS)]),
    ]
    barrier = pltpu.get_barrier_semaphore()
    for peer in peers:
        pl.semaphore_signal(barrier, inc=1, device_id=peer, device_id_type=MESH)
    pl.semaphore_wait(barrier, len(peers))

    mine = pl.ds(pl.multiple_of(FLAT + QUARTER * y, LANES), QUARTER)
    pieces = {"m": mine}
    for index in range(PIECES):
        pieces[index] = pl.ds(index * (FLAT // PIECES), FLAT // PIECES)

    def row(dxl, dz):
        return dxl * GROUP + (dz % NZ) * SPAN

    z_copies, x_copies, y_copies = {}, {}, ([], [])

    def along_z(piece, step, way):
        dz, cols = -way * step, pieces[piece]
        first, count = (0 if way > 0 else HALF, HALF) if step == 3 else (0, SPAN)
        here = pl.ds(row(0, dz) + first, count)
        there = pl.ds(row(0, dz - way) + first, count)
        target = by_z[1 if way > 0 else NZ - 1]
        z_copies[piece, step + 1, way] = remote(ws.at[here, cols], ws.at[there, cols], target)

    def along_x(piece, dz):
        cols = pieces[piece]
        copies = []
        for d, first in ((1, 0), (3, HALF)):
            here = pl.ds(row(0, dz) + first, HALF)
            there = pl.ds(row(1, dz) + first, HALF)
            copies.append(remote(ws.at[here, cols], ws.at[there, cols], by_x[d]))
        x_copies[piece, dz] = copies

    def along_y(dxl, dz):
        here = ws.at[pl.ds(row(dxl, dz), SPAN), mine]
        for d in (1, 3, 2):
            y_copies[dxl].append(remote(here, here, by_y[d]))

    def arrived_here(copies):
        for copy in copies:
            copy.wait()

    def arrived(copies):
        for copy in copies:
            copy.wait_recv()

    own_block.wait()
    for piece in ('m', 0, 1):
        for way in (1, -1):
            along_z(piece, 0, way)
        along_x(piece, 0)
    to_sibling = [
        remote(candidates, buf["cs"].at[pl.ds(ROWS, ROWS)], sibling),
        remote(scores, buf["rs"].at[pl.ds(ROWS, ROWS)], sibling),
        remote(queries, qs.at[pl.ds(ROWS, ROWS)], sibling),
    ]
    x_done = set()

    def from_x(piece, dz):
        arrived(x_copies[piece, dz])
        x_done.add((piece, dz))
        if piece == "m":
            along_y(1, dz)

    cs, rs, ts = buf["cs"], buf["rs"], buf["ts"]
    lane = lax.broadcasted_iota(jnp.int32, (ROWS, LANES), 1)
    entropy = []

    def teach(rows):
        raw = rs[rows]
        shifted = raw - jnp.max(raw, axis=1, keepdims=True)
        log_teacher = shifted - jnp.log(jnp.sum(jnp.exp(shifted), axis=1, keepdims=True))
        value = jnp.exp(log_teacher)
        ts[rows] = value
        entropy.append(jnp.sum(value * log_teacher, axis=1, keepdims=True))

    def spread(rows, chunk):
        chosen = cs[rows]
        slot = lane // SPAN + chunk * (LANES // SPAN)
        dxl, dz = slot // NZ, slot % NZ
        owner = (((z + dz) % NZ) * 2 + (x + dxl) % 2) * 2 + core
        target = owner * SPAN + lane % SPAN
        position = jnp.zeros((ROWS, LANES), jnp.int32)
        for step in (64, 32, 16, 8, 4, 2, 1):
            probe = jnp.take_along_axis(chosen, position + (step - 1), axis=1)
            position = jnp.where(probe < target, position + step, position)
        hit = jnp.take_along_axis(chosen, position, axis=1) == target
        value = jnp.take_along_axis(ts[rows], position, axis=1)
        tt[rows, chunk * LANES : (chunk + 1) * LANES] = jnp.where(hit, value, -1.0)

    own, other = pl.ds(0, ROWS), pl.ds(ROWS, ROWS)
    chores = [lambda: (arrived_here(own_teacher), teach(own))]
    chores += [lambda chunk=chunk: spread(own, chunk) for chunk in range(POOL // LANES)]
    chores += [lambda: (arrived(to_sibling[:2]), teach(other))]
    chores += [lambda chunk=chunk: spread(other, chunk) for chunk in range(POOL // LANES)]

    for piece, step in GATHER_ORDER:
        if piece == "x":
            for dz in ((0,) if step == 0 else (4,) if step == 4 else (-step, step)):
                from_x("m", dz)
            continue
        for way in (1, -1):
            z_copies[piece, step, way].wait_recv()
            if step < 4:
                along_z(piece, step, way)
                along_x(piece, -way * step)
                if piece == "m":
                    along_y(0, -way * step)
        if step == 4:
            along_x(piece, 4)
            if piece == "m":
                along_y(0, 4)
        if chores and (piece, step) != ("m", 1):
            chores.pop(0)()
    for chore in chores:
        chore()
    def dot_rows(a, b):
        return lax.dot_general(a, b, (((1,), (1,)), ((), ())), preferred_element_type=F32)

    column = lax.broadcasted_iota(jnp.int32, (2 * ROWS, W2), 1)
    own_queries.wait()
    arrived(to_sibling[2:])
    for dxl in range(2):
        if dxl == 1:
            for key in x_copies:
                if key not in x_done:
                    from_x(*key)
        arrived(y_copies[dxl])
        if dxl == 1:
            pass
        rows = pl.ds(dxl * GROUP, GROUP)
        head = qs[:, 0:W2]
        zero = jnp.zeros_like(head)
        narrow = ws[rows, 0:W2]
        level = dot_rows(jnp.where(column < W1, head, zero), narrow)
        lv[0, :, rows] = level
        level += dot_rows(jnp.where(column < W1, zero, head), narrow)
        lv[1, :, rows] = level
        level += dot_rows(qs[:, W2:W3], ws[rows, W2:W3])
        lv[2, :, rows] = level

        def score_step(index, total, rows=rows):
            cols = pl.ds(pl.multiple_of(index * 1024, 1024), 1024)
            return total + dot_rows(qs[:, cols], ws[rows, cols])

        lv[3, :, rows] = lax.fori_loop(1, E // 1024, score_step, level)


    scales = [1.0 / math.sqrt(width) for width in WIDTHS]
    strip_lane = lax.broadcasted_iota(jnp.int32, (STRIP, LANES), 1)

    def tabulate(columns):
        table = jnp.zeros((STRIP, LANES), F32)
        for index, value in enumerate(columns):
            table = jnp.where(strip_lane == index, value, table)
        return table

    def gather_terms(first):
        rows = pl.ds(first, STRIP)
        teacher_or = tt[rows]
        chosen = teacher_or >= 0.0
        teacher = jnp.where(chosen, teacher_or, 0.0)
        tops, sums, parts = [], [], []
        for level in range(4):
            logits = lv[level, rows] * scales[level]
            top = jnp.max(jnp.where(chosen, logits, -BIG), axis=1, keepdims=True)
            shifted = jnp.where(chosen, logits - top, 0.0)
            weight = jnp.where(chosen, jnp.exp(shifted), 0.0)
            lv[level, rows] = weight
            tops.append(top)
            sums.append(jnp.sum(weight, axis=1, keepdims=True))
            parts.append(jnp.sum(teacher * shifted, axis=1, keepdims=True))
        parts.append(jnp.sum(teacher, axis=1, keepdims=True))
        st[0, rows] = tabulate(tops)
        st[1, rows] = tabulate(sums)
        st[2, rows] = tabulate(parts)

    stats_copies = []
    for half in range(2):
        for first in range(half * ROWS, (half + 1) * ROWS, STRIP):
            gather_terms(first)
        here, there = pl.ds(half * ROWS, ROWS), pl.ds((1 - half) * ROWS, ROWS)
        stats_copies.append(remote(st.at[:, here], sr.at[:, there], sibling))

    loss_strips = []

    def finish_terms(first):
        rows = pl.ds(first, STRIP)
        top, top_other = st[0, rows], sr[0, rows]
        peak = jnp.maximum(top, top_other)
        fade, fade_other = jnp.exp(top - peak), jnp.exp(top_other - peak)
        total = st[1, rows] * fade + sr[1, rows] * fade_other
        factor = fade / total
        if first < ROWS:
            weight, weight_other = st[2, rows][:, 4:5], sr[2, rows][:, 4:5]
            part = st[2, rows] + weight * (top - peak) + sr[2, rows] + weight_other * (top_other - peak)
            terms = jnp.log(total) * (weight + weight_other) - part
            loss_strips.append(
                jnp.sum(jnp.where(strip_lane < 4, terms, 0.0), axis=1, keepdims=True)
            )
        teacher = jnp.maximum(tt[rows], 0.0)
        tail = None
        for level in (3, 2, 1, 0):
            dlogit = (lv[level, rows] * factor[:, level : level + 1] - teacher) * scales[level]
            tail = dlogit if tail is None else dlogit + tail
            grid[level, rows] = tail.astype(BF16)

    for half in (1, 0):
        stats_copies[1 - half].wait_recv()
        for first in range(half * ROWS, (half + 1) * ROWS, STRIP):
            finish_terms(first)


    pa, pab, pb, pbb, pc, pcb = (buf[k] for k in ("pa", "pab", "pb", "pbb", "pc", "pcb"))

    def dot_columns(a, b):
        return lax.dot_general(a, b, (((0,), (0,)), ((), ())), preferred_element_type=F32)

    def keep(dxl, q, result):
        rounded = result.astype(BF16)
        xh_of, y_of = q // 4, q % 4
        for dz in range(NZ):
            top = slice(dz * SPAN, dz * SPAN + HALF)
            low = slice(dz * SPAN + HALF, (dz + 1) * SPAN)
            whole = slice(dz * SPAN, (dz + 1) * SPAN)
            pa[dz, dxl, q] = result[whole, :WA]
            pab[dz, dxl, q] = rounded[whole, :WA]
            at = (dz - FIRST_Z) % NZ
            pb[dxl, xh_of, y_of, at] = result[top, WA:]
            pbb[dxl, xh_of, y_of, at] = rounded[top, WA:]
            pc[y_of, dxl, xh_of, at] = result[low, WA:]
            pcb[y_of, dxl, xh_of, at] = rounded[low, WA:]

    for dxl in range(2):
        part = pl.ds(dxl * GROUP, GROUP)
        narrow = lax.broadcasted_iota(jnp.int32, (GROUP, W2), 1) < W1
        first = qs[:, 0:W2]
        first = jnp.where(
            narrow, dot_columns(grid[0, :, part], first), dot_columns(grid[1, :, part], first)
        )
        second = dot_columns(grid[2, :, part], qs[:, W2:BLOCK])
        keep(dxl, 0, jnp.concatenate([first, second], axis=1))
        keep(dxl, 1, dot_columns(grid[2, :, part], qs[:, BLOCK : 2 * BLOCK]))
        for q in range(2, 8):
            keep(dxl, q, dot_columns(grid[3, :, part], qs[:, q * BLOCK : (q + 1) * BLOCK]))


    ra, rax, ray, fa, ga = (buf[k] for k in ("ra", "rax", "ray", "fa", "ga"))

    def ring(way, step, dxl):
        dz = (way * (5 - step)) % NZ
        target = by_z[1 if way > 0 else NZ - 1]
        slot = ra.at[0 if way > 0 else 1, step - 1, dxl]
        if step == 1:
            rows = pl.ds(0 if way > 0 else HALF, HALF)
            return remote(pab.at[dz, dxl, :, rows], slot.at[:, rows], target)
        return remote(pab.at[dz, dxl], slot, target)

    def toward(d):
        return ((x + d) % NX) // 2

    rings = {(way, dxl): ring(way, 1, dxl) for dxl in range(2) for way in (1, -1)}
    gb, gbb, rbx, rby = (buf[k] for k in ("gb", "gbb", "rbx", "rby"))
    gc, gcb, rcy, rcx = (buf[k] for k in ("gc", "gcb", "rcy", "rcx"))
    rbr, rcr = buf["rbr"], buf["rcr"]
    b_far, c_far, b_copies, c_copies = [], [], [[], []], [[], []]

    def opposite(chunk):
        part = pl.ds(*CHUNKS[chunk])
        for copies, ring_of, source, sink in (
            (b_far, by_x, lambda h: pbb.at[0, toward(2), pl.ds(2 * h, 2), part], rbr),
            (c_far, by_y, lambda h: pcb.at[(y + 2) % NY, h, :, part], rcr),
        ):
            copies.append(
                [remote(source(h), sink.at[h, :, part], ring_of[1 + 2 * h]) for h in (0, 1)]
            )

    def direct(chunk):
        part = pl.ds(*CHUNKS[chunk])
        for h, d in ((1, 1), (0, 3)):
            b_copies[chunk].append(
                remote(
                    pbb.at[1, toward(d), pl.ds(2 * h, 2), part],
                    rbx.at[1 - h, pl.ds(2 * h, 2), part],
                    by_x[d],
                )
            )
            c_copies[chunk].append(
                remote(pcb.at[(y + d) % NY, h, :, part], rcy.at[1 - h, h, :, part], by_y[d])
            )

    def relay(chunk):
        part = pl.ds(*CHUNKS[chunk])
        arrived(b_far[chunk])
        for h, d in ((0, 1), (1, 3)):
            half = pl.ds(2 * h, 2)
            total = pb[1, toward(d), half, part] + rbr[h, :, part].astype(F32)
            pbb[1, toward(d), half, part] = total.astype(BF16)
            b_copies[chunk].append(
                remote(pbb.at[1, toward(d), half, part], rbx.at[h, half, part], by_x[d])
            )
        arrived(c_far[chunk])
        for h, d in ((0, 1), (1, 3)):
            to = (y + d) % NY
            total = pc[to, h, :, part] + rcr[h, :, part].astype(F32)
            pcb[to, h, :, part] = total.astype(BF16)
            c_copies[chunk].append(
                remote(pcb.at[to, h, :, part], rcy.at[h, h, :, part], by_y[d])
            )

    opposite(0)
    direct(0)

    diagonal = lax.broadcasted_iota(jnp.int32, (ROWS, LANES), 0) == lax.broadcasted_iota(
        jnp.int32, (ROWS, LANES), 1
    )
    loss_rows = 4.0 * entropy[0] + jnp.concatenate(loss_strips, axis=0)
    loss[...] = jnp.sum(jnp.where(diagonal, loss_rows, 0.0), axis=0, keepdims=True)

    def dot_plain(a, b):
        return jnp.dot(a, b, preferred_element_type=F32)

    def keep_query(cols, result):
        go[:, cols] = result[:ROWS]
        gs[:, cols] = result[ROWS:]

    first = ws[:, 0:W2]
    keep_query(
        slice(0, W2), jnp.where(column < W1, dot_plain(grid[0], first), dot_plain(grid[1], first))
    )
    keep_query(slice(W2, BLOCK), dot_plain(grid[2], ws[:, W2:BLOCK]))
    keep_query(slice(BLOCK, W3), dot_plain(grid[2], ws[:, BLOCK:W3]))

    def query_step(index, carry):
        cols = pl.ds(pl.multiple_of(index * BLOCK, BLOCK), BLOCK)
        keep_query(cols, dot_plain(grid[3], ws[:, cols]))
        return carry


    def ring_step(step):
        for dxl in range(2):
            for way in (1, -1):
                rings[way, dxl].wait_recv()
                dz = (way * (4 - step)) % NZ
                slot = ra.at[0 if way > 0 else 1, step - 1, dxl]
                rows = pl.ds(0, SPAN)
                if step == 1:
                    rows = pl.ds(0 if way > 0 else HALF, HALF)
                pab[dz, dxl, :, rows] = (pa[dz, dxl, :, rows] + slot[:, rows].astype(F32)).astype(
                    BF16
                )
                rings[way, dxl] = ring(way, step + 1, dxl)

    def ring_end():
        for dxl in range(2):
            rings[1, dxl].wait_recv()
            rings[-1, dxl].wait_recv()
            total = pa[0, dxl] + ra[0, 3, dxl].astype(F32) + ra[1, 3, dxl].astype(F32)
            fa[dxl] = total.reshape(2, 4, SPAN, WA)
        return [remote(fa.at[d % 2, toward(d)], rax.at[d - 1], by_x[d]) for d in (1, 2, 3)]

    def three(own, parts):
        return own + parts[0].astype(F32) + parts[1].astype(F32) + parts[2].astype(F32)

    def b_second(chunk):
        part = pl.ds(*CHUNKS[chunk])
        arrived(b_copies[chunk])
        total = pb[0, xh, :, part] + rbx[0, :, part].astype(F32) + rbx[1, :, part].astype(F32)
        gb[:, part] = total
        gbb[:, part] = total.astype(BF16)
        return [
            remote(gbb.at[(y + d) % NY, part], rby.at[d - 1, part], by_y[d]) for d in (2, 1, 3)
        ]

    def c_second(chunk):
        part = pl.ds(*CHUNKS[chunk])
        arrived(c_copies[chunk])
        total = pc[y, :, :, part] + rcy[0, :, :, part].astype(F32)
        total += rcy[1, :, :, part].astype(F32)
        gc[:, :, part] = total
        gcb[:, :, part] = total.astype(BF16)
        return [
            remote(gcb.at[d % 2, toward(d), part], rcx.at[d - 1, part], by_x[d]) for d in (2, 1, 3)
        ]

    def third(chunk, total, wide, narrow, wide_in, narrow_in):
        start, count = CHUNKS[chunk]
        wide[pl.ds(start, count)] = total
        narrow[pl.ds(start, count)] = total.astype(BF16)
        copies = []
        for at in range(start, start + count):
            dz = (at + FIRST_Z) % NZ
            if dz in FAR:
                copies.append(remote(narrow.at[at], narrow_in.at[at], by_z[dz]))
            elif dz:
                copies.append(remote(wide.at[at], wide_in.at[at], by_z[dz]))
        return copies

    hb, hbb, rbz, rbzb = (buf[k] for k in ("hb", "hbb", "rbz", "rbzb"))
    hc, hcb, rcz, rczb = (buf[k] for k in ("hc", "hcb", "rcz", "rczb"))

    def b_third(chunk):
        part = pl.ds(*CHUNKS[chunk])
        arrived(b_next[chunk])
        return third(chunk, three(gb[y, part], rby[:, part]), hb, hbb, rbz, rbzb)

    def c_third(chunk):
        part = pl.ds(*CHUNKS[chunk])
        arrived(c_next[chunk])
        return third(chunk, three(gc[0, xh, part], rcx[:, part]), hc, hcb, rcz, rczb)

    b_next, c_next, last_copies = [None, None], [None, None], []
    relay(0)
    opposite(1)
    direct(1)
    ring_step(1)
    ring_step(2)
    lax.fori_loop(2, E // BLOCK, query_step, 0)
    query_copy = remote(gs, gr, sibling)
    b_next[0] = b_second(0)
    c_next[0] = c_second(0)
    ring_step(3)
    relay(1)
    last_copies += b_third(0)
    last_copies += c_third(0)
    ax_copies = ring_end()
    b_next[1] = b_second(1)
    c_next[1] = c_second(1)
    query_copy.wait_recv()
    go[...] += gr[...]
    out_copy = local(go, grad_queries)
    arrived(ax_copies)
    ga[...] = three(fa[0, xh], rax)
    ay_copies = [remote(ga.at[(y + d) % NY], ray.at[d - 1], by_y[d]) for d in (1, 2, 3)]
    last_copies += b_third(1)
    last_copies += c_third(1)
    arrived(ay_copies)
    ob = buf["ob"]
    ob[:, :WA] = three(ga[y], ray)
    arrived(last_copies)
    at_home = (0 - FIRST_Z) % NZ
    total_b, total_c = hb[at_home], hc[at_home]
    for at in range(NZ):
        if (at + FIRST_Z) % NZ in FAR:
            total_b += rbzb[at].astype(F32)
            total_c += rczb[at].astype(F32)
        elif at != at_home:
            total_b += rbz[at]
            total_c += rcz[at]
    ob[:HALF, WA:] = total_b
    ob[HALF:, WA:] = total_c
    last = local(ob, grad_passages)
    for copy in sent:
        copy.wait_send()
    out_copy.wait()
    last.wait()


def main_call(queries, passages, candidates, scores):
    scratch = [pltpu.VMEM(shape, dtype) for shape, dtype in SCRATCH.values()]
    scratch += [
        pltpu.SemaphoreType.DMA((N_REMOTE,)),
        pltpu.SemaphoreType.DMA((N_REMOTE,)),
        pltpu.SemaphoreType.DMA((N_LOCAL,)),
    ]
    anywhere = pl.BlockSpec(memory_space=pl.ANY)
    return pl.pallas_call(
        main_kernel,
        out_shape=(
            jax.ShapeDtypeStruct((1, ROWS), F32),
            jax.ShapeDtypeStruct((ROWS, E), F32),
            jax.ShapeDtypeStruct((SPAN, BLOCK), F32),
        ),
        in_specs=[anywhere] * 4,
        out_specs=(pl.BlockSpec(memory_space=pltpu.VMEM), anywhere, anywhere),
        scratch_shapes=scratch,
        compiler_params=pltpu.CompilerParams(
            collective_id=0, has_side_effects=True, vmem_limit_bytes=60 * 2**20
        ),
        name="distill",
    )(queries, passages, candidates, scores)


def finish_kernel(*refs):
    sources, sinks, stages, sems = refs[:3], refs[3:6], refs[6:9], refs[9]
    pieces = [(0, pl.ds(first, PIECE)) for first in range(0, ROWS, PIECE)]
    pieces += [(1, slice(None)), (2, slice(None))]
    loads, stores = [], []
    for index, (which, rows) in enumerate(pieces):
        source, stage, sink = sources[which], stages[which], sinks[which]
        loads.append(pltpu.make_async_copy(source.at[rows], stage.at[rows], sems.at[0, index]))
        stores.append(pltpu.make_async_copy(stage.at[rows], sink.at[rows], sems.at[1, index]))
    for copy in loads:
        copy.start()
    for load, store in zip(loads, stores):
        load.wait()
        store.start()
    for copy in stores:
        copy.wait()


def finish(*arrays):
    anywhere = pl.BlockSpec(memory_space=pl.ANY)
    return pl.pallas_call(
        finish_kernel,
        out_shape=tuple(jax.ShapeDtypeStruct(a.shape, a.dtype) for a in arrays),
        in_specs=[anywhere] * 3,
        out_specs=(anywhere,) * 3,
        scratch_shapes=[pltpu.VMEM(a.shape, a.dtype) for a in arrays]
        + [pltpu.SemaphoreType.DMA((2, ROWS // PIECE + 2))],
        compiler_params=pltpu.CompilerParams(vmem_limit_bytes=60 * 2**20),
        name="finish",
    )(*arrays)


def shards(queries, passages, candidates, teacher_scores):
    loss, grad_queries, grad_passages = main_call(queries, passages, candidates, teacher_scores)
    grad_queries, grad_passages, loss = finish(grad_queries, grad_passages, loss)
    return (loss.reshape(ROWS), grad_queries, grad_passages)


def solution(mesh):
    return jax.shard_map(
        shards,
        mesh=mesh,
        in_specs=(
            P(("query", "passage"), None),
            P("passage", None),
            P(("query", "passage"), None),
            P(("query", "passage"), None),
        ),
        out_specs=(P(("query", "passage")), P(("query", "passage"), None), P("passage", "query")),
        check_vma=False,
    )
```

```python
import functools
import math

import jax
import jax.numpy as jnp
from jax import lax
from jax.experimental import pallas as pl
from jax.experimental.pallas import tpu as pltpu
from jax.sharding import PartitionSpec as P

MESH = pl.DeviceIdType.MESH
BF16 = jnp.bfloat16
F32 = jnp.float32

E = 4096
W1, W2, W3 = 64, 256, 1024
WIDTHS = (W1, W2, W3, E)
ROWS = 128
SPAN = 32
HALF = 16
NX, NY, NZ = 4, 4, 8
POOL = 2 * NZ * SPAN
GROUP = NZ * SPAN
LANES = 128
BIG = 3.0e38
PIECE = 16
STRIP = 128

QUARTER = 384
FLAT = E - 4 * QUARTER
PIECES = 2
GATHER_ORDER = (
    ('m', 1), ('x', 0), (0, 1), (1, 1), ('m', 2), ('x', 1), (0, 2), (1, 2), ('m', 3), ('x', 2), (0, 3), (1, 3), ('m', 4), ('x', 3), (0, 4), (1, 4), ('x', 4)
)

BLOCK = 512
WA = 128
WB = BLOCK - WA
FIRST_Z = 2
CHUNKS = ((0, 5), (5, 3))
FAR = (3, 4, 5)


def place():
    query = lax.axis_index("query")
    passage = lax.axis_index("passage")
    x = (query // 4) * 2 + (passage // 2) % 2
    return x, query % 4, passage // 4, passage % 2


def device(x, y, z, core):
    x, y, z = x % NX, y % NY, z % NZ
    return ((x // 2) * 4 + y, (z * 2 + x % 2) * 2 + core)


SCRATCH = dict(
    qs=((2 * ROWS, E), BF16),
    ws=((2 * GROUP, E), BF16),
    cs=((2 * ROWS, LANES), jnp.int32),
    rs=((2 * ROWS, LANES), F32),
    ts=((2 * ROWS, LANES), F32),
    tt=((POOL, 2 * ROWS), F32),
    lv=((4, POOL, 2 * ROWS), F32),
    st=((2, 3, 8, ROWS), F32),
    sr=((2, 3, 8, ROWS), F32),
    grid=((4, POOL, 2 * ROWS), BF16),
    turned=((4, 2 * ROWS, POOL), BF16),
    go=((ROWS, E), F32),
    gs=((ROWS, E), F32),
    gr=((ROWS, E), F32),
    pa=((NZ, 2, 8, SPAN, WA), F32),
    pab=((NZ, 2, 8, SPAN, WA), BF16),
    ra=((2, 4, 2, 8, SPAN, WA), BF16),
    fa=((2, 2, 4, SPAN, WA), F32),
    rax=((3, 4, SPAN, WA), F32),
    ga=((4, SPAN, WA), F32),
    ray=((3, SPAN, WA), F32),
    pb=((2, 2, 4, NZ, HALF, WB), F32),
    pbb=((2, 2, 4, NZ, HALF, WB), BF16),
    rbr=((2, 2, NZ, HALF, WB), BF16),
    rbx=((2, 4, NZ, HALF, WB), BF16),
    gb=((4, NZ, HALF, WB), F32),
    gbb=((4, NZ, HALF, WB), BF16),
    rby=((3, NZ, HALF, WB), BF16),
    hb=((NZ, HALF, WB), F32),
    hbb=((NZ, HALF, WB), BF16),
    rbz=((NZ, HALF, WB), F32),
    rbzb=((NZ, HALF, WB), BF16),
    pc=((4, 2, 2, NZ, HALF, WB), F32),
    pcb=((4, 2, 2, NZ, HALF, WB), BF16),
    rcr=((2, 2, NZ, HALF, WB), BF16),
    rcy=((2, 2, 2, NZ, HALF, WB), BF16),
    gc=((2, 2, NZ, HALF, WB), F32),
    gcb=((2, 2, NZ, HALF, WB), BF16),
    rcx=((3, NZ, HALF, WB), BF16),
    hc=((NZ, HALF, WB), F32),
    hcb=((NZ, HALF, WB), BF16),
    rcz=((NZ, HALF, WB), F32),
    rczb=((NZ, HALF, WB), BF16),
    ob=((SPAN, BLOCK), F32),
)
N_REMOTE = 260
N_LOCAL = 16


def main_kernel(queries, passages, candidates, scores, loss, grad_queries, grad_passages, *scratch):
    buf = dict(zip(SCRATCH, scratch))
    send_sems, recv_sems, local_sems = scratch[len(SCRATCH) :]
    qs, ws, tt, lv, st, sr, grid = (buf[k] for k in ("qs", "ws", "tt", "lv", "st", "sr", "grid"))
    go, gs, gr = (buf[k] for k in ("go", "gs", "gr"))
    x, y, z, core = place()
    xh = x // 2
    used = [0, 0]
    sent = []

    def remote(src, dst, target):
        index = used[0]
        used[0] += 1
        copy = pltpu.make_async_remote_copy(
            src_ref=src,
            dst_ref=dst,
            send_sem=send_sems.at[index],
            recv_sem=recv_sems.at[index],
            device_id=target,
            device_id_type=MESH,
        )
        copy.start()
        sent.append(copy)
        return copy

    def local(src, dst):
        index = used[1]
        used[1] += 1
        copy = pltpu.make_async_copy(src, dst, local_sems.at[index])
        copy.start()
        return copy

    sibling = device(x, y, z, 1 - core)
    by_x = {d: device(x + d, y, z, core) for d in (1, 2, 3)}
    by_y = {d: device(x, y + d, z, core) for d in (1, 2, 3)}
    by_z = {d: device(x, y, z + d, core) for d in range(1, NZ)}
    peers = [sibling, *by_x.values(), *by_y.values(), by_z[1], by_z[NZ - 1]]

    own_block = local(passages, ws.at[pl.ds(0, SPAN)])
    own_queries = local(queries, qs.at[pl.ds(0, ROWS)])
    own_teacher = [
        local(candidates, buf["cs"].at[pl.ds(0, ROWS)]),
        local(scores, buf["rs"].at[pl.ds(0, ROWS)]),
    ]
    barrier = pltpu.get_barrier_semaphore()
    for peer in peers:
        pl.semaphore_signal(barrier, inc=1, device_id=peer, device_id_type=MESH)
    pl.semaphore_wait(barrier, len(peers))

    mine = pl.ds(pl.multiple_of(FLAT + QUARTER * y, LANES), QUARTER)
    pieces = {"m": mine}
    for index in range(PIECES):
        pieces[index] = pl.ds(index * (FLAT // PIECES), FLAT // PIECES)

    def row(dxl, dz):
        return dxl * GROUP + (dz % NZ) * SPAN

    z_copies, x_copies, y_copies = {}, {}, ([], [])

    def along_z(piece, step, way):
        dz, cols = -way * step, pieces[piece]
        first, count = (0 if way > 0 else HALF, HALF) if step == 3 else (0, SPAN)
        here = pl.ds(row(0, dz) + first, count)
        there = pl.ds(row(0, dz - way) + first, count)
        target = by_z[1 if way > 0 else NZ - 1]
        z_copies[piece, step + 1, way] = remote(ws.at[here, cols], ws.at[there, cols], target)

    def along_x(piece, dz):
        cols = pieces[piece]
        copies = []
        for d, first in ((1, 0), (3, HALF)):
            here = pl.ds(row(0, dz) + first, HALF)
            there = pl.ds(row(1, dz) + first, HALF)
            copies.append(remote(ws.at[here, cols], ws.at[there, cols], by_x[d]))
        x_copies[piece, dz] = copies

    def along_y(dxl, dz):
        here = ws.at[pl.ds(row(dxl, dz), SPAN), mine]
        for d in (1, 3, 2):
            y_copies[dxl].append(remote(here, here, by_y[d]))

    def arrived_here(copies):
        for copy in copies:
            copy.wait()

    def arrived(copies):
        for copy in copies:
            copy.wait_recv()

    own_block.wait()
    for piece in ('m', 0, 1):
        for way in (1, -1):
            along_z(piece, 0, way)
        along_x(piece, 0)
    to_sibling = [
        remote(candidates, buf["cs"].at[pl.ds(ROWS, ROWS)], sibling),
        remote(scores, buf["rs"].at[pl.ds(ROWS, ROWS)], sibling),
        remote(queries, qs.at[pl.ds(ROWS, ROWS)], sibling),
    ]
    x_done = set()

    def from_x(piece, dz):
        arrived(x_copies[piece, dz])
        x_done.add((piece, dz))
        if piece == "m":
            along_y(1, dz)

    cs, rs, ts = buf["cs"], buf["rs"], buf["ts"]
    lane = lax.broadcasted_iota(jnp.int32, (ROWS, LANES), 1)
    entropy = []

    def teach(rows):
        raw = rs[rows]
        shifted = raw - jnp.max(raw, axis=1, keepdims=True)
        log_teacher = shifted - jnp.log(jnp.sum(jnp.exp(shifted), axis=1, keepdims=True))
        value = jnp.exp(log_teacher)
        ts[rows] = value
        entropy.append(jnp.sum(value * log_teacher, axis=1, keepdims=True))

    def spread(rows, chunk):
        chosen = cs[rows]
        slot = lane // SPAN + chunk * (LANES // SPAN)
        dxl, dz = slot // NZ, slot % NZ
        owner = (((z + dz) % NZ) * 2 + (x + dxl) % 2) * 2 + core
        target = owner * SPAN + lane % SPAN
        position = jnp.zeros((ROWS, LANES), jnp.int32)
        for step in (64, 32, 16, 8, 4, 2, 1):
            probe = jnp.take_along_axis(chosen, position + (step - 1), axis=1)
            position = jnp.where(probe < target, position + step, position)
        hit = jnp.take_along_axis(chosen, position, axis=1) == target
        value = jnp.take_along_axis(ts[rows], position, axis=1)
        tt[chunk * LANES : (chunk + 1) * LANES, rows] = jnp.where(hit, value, -1.0).T

    own, other = pl.ds(0, ROWS), pl.ds(ROWS, ROWS)
    chores = [lambda: (arrived_here(own_teacher), teach(own))]
    chores += [lambda chunk=chunk: spread(own, chunk) for chunk in range(POOL // LANES)]
    chores += [lambda: (arrived(to_sibling[:2]), teach(other))]
    chores += [lambda chunk=chunk: spread(other, chunk) for chunk in range(POOL // LANES)]

    for piece, step in GATHER_ORDER:
        if piece == "x":
            for dz in ((0,) if step == 0 else (4,) if step == 4 else (-step, step)):
                from_x("m", dz)
            continue
        for way in (1, -1):
            z_copies[piece, step, way].wait_recv()
            if step < 4:
                along_z(piece, step, way)
                along_x(piece, -way * step)
                if piece == "m":
                    along_y(0, -way * step)
        if step == 4:
            along_x(piece, 4)
            if piece == "m":
                along_y(0, 4)
        if chores and (piece, step) != ("m", 1):
            chores.pop(0)()
    for chore in chores:
        chore()
    def dot_rows(a, b):
        return lax.dot_general(a, b, (((1,), (1,)), ((), ())), preferred_element_type=F32)

    column = lax.broadcasted_iota(jnp.int32, (2 * ROWS, W2), 1)
    own_queries.wait()
    arrived(to_sibling[2:])
    for dxl in range(2):
        if dxl == 1:
            for key in x_copies:
                if key not in x_done:
                    from_x(*key)
        arrived(y_copies[dxl])
        rows = pl.ds(dxl * GROUP, GROUP)
        head = qs[:, 0:W2]
        zero = jnp.zeros_like(head)
        narrow = ws[rows, 0:W2]
        level = dot_rows(narrow, jnp.where(column < W1, head, zero))
        lv[0, rows] = level
        level += dot_rows(narrow, jnp.where(column < W1, zero, head))
        lv[1, rows] = level
        level += dot_rows(ws[rows, W2:W3], qs[:, W2:W3])
        lv[2, rows] = level

        def score_step(index, total, rows=rows):
            cols = pl.ds(pl.multiple_of(index * 1024, 1024), 1024)
            return total + dot_rows(ws[rows, cols], qs[:, cols])

        lv[3, rows] = lax.fori_loop(1, E // 1024, score_step, level)


    scales = [1.0 / math.sqrt(width) for width in WIDTHS]
    strips = [pl.ds(first, STRIP) for first in range(0, POOL, STRIP)]

    def tabulate(rows):
        rows = rows + [jnp.zeros((1, ROWS), F32)] * (8 - len(rows))
        return jnp.concatenate(rows, axis=0)

    def gather_terms(half):
        lanes = pl.ds(half * ROWS, ROWS)
        tops, sums, parts = [], [], []
        weight_sum = jnp.zeros((1, ROWS), F32)
        for strip in strips:
            weight_sum += jnp.sum(jnp.maximum(tt[strip, lanes], 0.0), axis=0, keepdims=True)
        for level in range(4):
            top = jnp.full((1, ROWS), -BIG, F32)
            for strip in strips:
                logits = jnp.where(
                    tt[strip, lanes] >= 0.0, lv[level, strip, lanes] * scales[level], -BIG
                )
                lv[level, strip, lanes] = logits
                top = jnp.maximum(top, jnp.max(logits, axis=0, keepdims=True))
            total = jnp.zeros((1, ROWS), F32)
            part = jnp.zeros((1, ROWS), F32)
            for strip in strips:
                shifted = lv[level, strip, lanes] - top
                weight = jnp.exp(shifted)
                lv[level, strip, lanes] = weight
                total += jnp.sum(weight, axis=0, keepdims=True)
                teacher = jnp.maximum(tt[strip, lanes], 0.0)
                part += jnp.sum(teacher * shifted, axis=0, keepdims=True)
            tops.append(top)
            sums.append(total)
            parts.append(part)
        st[half, 0] = tabulate(tops)
        st[half, 1] = tabulate(sums)
        st[half, 2] = tabulate(parts + [weight_sum])

    stats_copies = []
    for half in range(2):
        gather_terms(half)
        stats_copies.append(remote(st.at[half], sr.at[1 - half], sibling))

    loss_terms = []

    def finish_terms(half):
        lanes = pl.ds(half * ROWS, ROWS)
        top, top_other = st[half, 0], sr[half, 0]
        peak = jnp.maximum(top, top_other)
        fade, fade_other = jnp.exp(top - peak), jnp.exp(top_other - peak)
        total = st[half, 1] * fade + sr[half, 1] * fade_other
        factor = fade / total
        if half == 0:
            part, part_other = st[half, 2], sr[half, 2]
            weight, weight_other = part[4:5], part_other[4:5]
            part = part + weight * (top - peak) + part_other + weight_other * (top_other - peak)
            terms = jnp.log(total) * (weight + weight_other) - part
            loss_terms.append(jnp.sum(terms[:4], axis=0, keepdims=True))
        for strip in strips:
            teacher = jnp.maximum(tt[strip, lanes], 0.0)
            tail = None
            for level in (3, 2, 1, 0):
                student = lv[level, strip, lanes] * factor[level : level + 1]
                dlogit = (student - teacher) * scales[level]
                tail = dlogit if tail is None else dlogit + tail
                grid[level, strip, lanes] = tail.astype(BF16)

    for half in (1, 0):
        stats_copies[1 - half].wait_recv()
        finish_terms(half)


    pa, pab, pb, pbb, pc, pcb = (buf[k] for k in ("pa", "pab", "pb", "pbb", "pc", "pcb"))

    def dot_plain(a, b):
        return jnp.dot(a, b, preferred_element_type=F32)

    def keep(dxl, q, result):
        rounded = result.astype(BF16)
        xh_of, y_of = q // 4, q % 4
        for dz in range(NZ):
            top = slice(dz * SPAN, dz * SPAN + HALF)
            low = slice(dz * SPAN + HALF, (dz + 1) * SPAN)
            whole = slice(dz * SPAN, (dz + 1) * SPAN)
            pa[dz, dxl, q] = result[whole, :WA]
            pab[dz, dxl, q] = rounded[whole, :WA]
            at = (dz - FIRST_Z) % NZ
            pb[dxl, xh_of, y_of, at] = result[top, WA:]
            pbb[dxl, xh_of, y_of, at] = rounded[top, WA:]
            pc[y_of, dxl, xh_of, at] = result[low, WA:]
            pcb[y_of, dxl, xh_of, at] = rounded[low, WA:]

    ra, rax, ray, fa, ga = (buf[k] for k in ("ra", "rax", "ray", "fa", "ga"))

    def ring(way, step, dxl):
        dz = (way * (5 - step)) % NZ
        target = by_z[1 if way > 0 else NZ - 1]
        slot = ra.at[0 if way > 0 else 1, step - 1, dxl]
        if step == 1:
            rows = pl.ds(0 if way > 0 else HALF, HALF)
            return remote(pab.at[dz, dxl, :, rows], slot.at[:, rows], target)
        return remote(pab.at[dz, dxl], slot, target)

    def toward(d):
        return ((x + d) % NX) // 2

    rings = {}
    gb, gbb, rbx, rby = (buf[k] for k in ("gb", "gbb", "rbx", "rby"))
    gc, gcb, rcy, rcx = (buf[k] for k in ("gc", "gcb", "rcy", "rcx"))
    rbr, rcr = buf["rbr"], buf["rcr"]
    b_far, c_far, b_copies, c_copies = [], [], [[], []], [[], []]

    def opposite_b(chunk):
        part = pl.ds(*CHUNKS[chunk])
        b_far.append(
            [
                remote(pbb.at[0, toward(2), pl.ds(2 * h, 2), part], rbr.at[h, :, part], by_x[d])
                for h, d in ((0, 1), (1, 3))
            ]
        )

    def opposite_c(chunk):
        part = pl.ds(*CHUNKS[chunk])
        c_far.append(
            [
                remote(pcb.at[(y + 2) % NY, h, :, part], rcr.at[h, :, part], by_y[d])
                for h, d in ((0, 1), (1, 3))
            ]
        )

    def direct(chunk):
        part = pl.ds(*CHUNKS[chunk])
        for h, d in ((1, 1), (0, 3)):
            b_copies[chunk].append(
                remote(
                    pbb.at[1, toward(d), pl.ds(2 * h, 2), part],
                    rbx.at[1 - h, pl.ds(2 * h, 2), part],
                    by_x[d],
                )
            )
            c_copies[chunk].append(
                remote(pcb.at[(y + d) % NY, h, :, part], rcy.at[1 - h, h, :, part], by_y[d])
            )

    def relay(chunk):
        part = pl.ds(*CHUNKS[chunk])
        arrived(b_far[chunk])
        for h, d in ((0, 1), (1, 3)):
            half = pl.ds(2 * h, 2)
            total = pb[1, toward(d), half, part] + rbr[h, :, part].astype(F32)
            pbb[1, toward(d), half, part] = total.astype(BF16)
            b_copies[chunk].append(
                remote(pbb.at[1, toward(d), half, part], rbx.at[h, half, part], by_x[d])
            )
        arrived(c_far[chunk])
        for h, d in ((0, 1), (1, 3)):
            to = (y + d) % NY
            total = pc[to, h, :, part] + rcr[h, :, part].astype(F32)
            pcb[to, h, :, part] = total.astype(BF16)
            c_copies[chunk].append(
                remote(pcb.at[to, h, :, part], rcy.at[h, h, :, part], by_y[d])
            )

    for dxl in range(2):
        part = pl.ds(dxl * GROUP, GROUP)
        narrow = lax.broadcasted_iota(jnp.int32, (GROUP, W2), 1) < W1
        first = qs[:, 0:W2]
        first = jnp.where(
            narrow, dot_plain(grid[0, part], first), dot_plain(grid[1, part], first)
        )
        second = dot_plain(grid[2, part], qs[:, W2:BLOCK])
        keep(dxl, 0, jnp.concatenate([first, second], axis=1))
        keep(dxl, 1, dot_plain(grid[2, part], qs[:, BLOCK : 2 * BLOCK]))
        for q in range(2, 8):
            keep(dxl, q, dot_plain(grid[3, part], qs[:, q * BLOCK : (q + 1) * BLOCK]))
        for way in (1, -1):
            rings[way, dxl] = ring(way, 1, dxl)
        if dxl == 0:
            opposite_b(0)
    opposite_c(0)
    direct(0)

    diagonal = lax.broadcasted_iota(jnp.int32, (ROWS, LANES), 0) == lax.broadcasted_iota(
        jnp.int32, (ROWS, LANES), 1
    )
    entropy_row = jnp.sum(jnp.where(diagonal, entropy[0], 0.0), axis=0, keepdims=True)
    loss[...] = 4.0 * entropy_row + loss_terms[0]

    turned = buf["turned"]
    for level in range(4):
        turned[level] = grid[level].T

    def keep_query(cols, result):
        go[:, cols] = result[:ROWS]
        gs[:, cols] = result[ROWS:]

    first = ws[:, 0:W2]
    keep_query(
        slice(0, W2), jnp.where(column < W1, dot_plain(turned[0], first), dot_plain(turned[1], first))
    )
    keep_query(slice(W2, BLOCK), dot_plain(turned[2], ws[:, W2:BLOCK]))
    keep_query(slice(BLOCK, W3), dot_plain(turned[2], ws[:, BLOCK:W3]))

    def query_step(index, carry):
        cols = pl.ds(pl.multiple_of(index * BLOCK, BLOCK), BLOCK)
        keep_query(cols, dot_plain(turned[3], ws[:, cols]))
        return carry


    def ring_step(step):
        for dxl in range(2):
            for way in (1, -1):
                rings[way, dxl].wait_recv()
                dz = (way * (4 - step)) % NZ
                slot = ra.at[0 if way > 0 else 1, step - 1, dxl]
                rows = pl.ds(0, SPAN)
                if step == 1:
                    rows = pl.ds(0 if way > 0 else HALF, HALF)
                pab[dz, dxl, :, rows] = (pa[dz, dxl, :, rows] + slot[:, rows].astype(F32)).astype(
                    BF16
                )
                rings[way, dxl] = ring(way, step + 1, dxl)

    def ring_end():
        for dxl in range(2):
            rings[1, dxl].wait_recv()
            rings[-1, dxl].wait_recv()
            total = pa[0, dxl] + ra[0, 3, dxl].astype(F32) + ra[1, 3, dxl].astype(F32)
            fa[dxl] = total.reshape(2, 4, SPAN, WA)
        return [remote(fa.at[d % 2, toward(d)], rax.at[d - 1], by_x[d]) for d in (1, 2, 3)]

    def three(own, parts):
        return own + parts[0].astype(F32) + parts[1].astype(F32) + parts[2].astype(F32)

    def b_second(chunk):
        part = pl.ds(*CHUNKS[chunk])
        arrived(b_copies[chunk])
        total = pb[0, xh, :, part] + rbx[0, :, part].astype(F32) + rbx[1, :, part].astype(F32)
        gb[:, part] = total
        gbb[:, part] = total.astype(BF16)
        return [
            remote(gbb.at[(y + d) % NY, part], rby.at[d - 1, part], by_y[d]) for d in (2, 1, 3)
        ]

    def c_second(chunk):
        part = pl.ds(*CHUNKS[chunk])
        arrived(c_copies[chunk])
        total = pc[y, :, :, part] + rcy[0, :, :, part].astype(F32)
        total += rcy[1, :, :, part].astype(F32)
        gc[:, :, part] = total
        gcb[:, :, part] = total.astype(BF16)
        return [
            remote(gcb.at[d % 2, toward(d), part], rcx.at[d - 1, part], by_x[d]) for d in (2, 1, 3)
        ]

    def third(chunk, total, wide, narrow, wide_in, narrow_in):
        start, count = CHUNKS[chunk]
        wide[pl.ds(start, count)] = total
        narrow[pl.ds(start, count)] = total.astype(BF16)
        copies = []
        for at in range(start, start + count):
            dz = (at + FIRST_Z) % NZ
            if dz in FAR:
                copies.append(remote(narrow.at[at], narrow_in.at[at], by_z[dz]))
            elif dz:
                copies.append(remote(wide.at[at], wide_in.at[at], by_z[dz]))
        return copies

    hb, hbb, rbz, rbzb = (buf[k] for k in ("hb", "hbb", "rbz", "rbzb"))
    hc, hcb, rcz, rczb = (buf[k] for k in ("hc", "hcb", "rcz", "rczb"))

    def b_third(chunk):
        part = pl.ds(*CHUNKS[chunk])
        arrived(b_next[chunk])
        return third(chunk, three(gb[y, part], rby[:, part]), hb, hbb, rbz, rbzb)

    def c_third(chunk):
        part = pl.ds(*CHUNKS[chunk])
        arrived(c_next[chunk])
        return third(chunk, three(gc[0, xh, part], rcx[:, part]), hc, hcb, rcz, rczb)

    b_next, c_next, last_copies = [None, None], [None, None], []
    relay(0)
    opposite_b(1)
    opposite_c(1)
    direct(1)
    ring_step(1)
    ring_step(2)
    lax.fori_loop(2, E // BLOCK, query_step, 0)
    query_copy = remote(gs, gr, sibling)
    b_next[0] = b_second(0)
    c_next[0] = c_second(0)
    ring_step(3)
    relay(1)
    last_copies += b_third(0)
    last_copies += c_third(0)
    ax_copies = ring_end()
    b_next[1] = b_second(1)
    c_next[1] = c_second(1)
    query_copy.wait_recv()
    go[...] += gr[...]
    out_copy = local(go, grad_queries)
    arrived(ax_copies)
    ga[...] = three(fa[0, xh], rax)
    ay_copies = [remote(ga.at[(y + d) % NY], ray.at[d - 1], by_y[d]) for d in (1, 2, 3)]
    last_copies += b_third(1)
    last_copies += c_third(1)
    arrived(ay_copies)
    ob = buf["ob"]
    ob[:, :WA] = three(ga[y], ray)
    arrived(last_copies)
    at_home = (0 - FIRST_Z) % NZ
    total_b, total_c = hb[at_home], hc[at_home]
    for at in range(NZ):
        if (at + FIRST_Z) % NZ in FAR:
            total_b += rbzb[at].astype(F32)
            total_c += rczb[at].astype(F32)
        elif at != at_home:
            total_b += rbz[at]
            total_c += rcz[at]
    ob[:HALF, WA:] = total_b
    ob[HALF:, WA:] = total_c
    last = local(ob, grad_passages)
    for copy in sent:
        copy.wait_send()
    out_copy.wait()
    last.wait()


def main_call(queries, passages, candidates, scores):
    scratch = [pltpu.VMEM(shape, dtype) for shape, dtype in SCRATCH.values()]
    scratch += [
        pltpu.SemaphoreType.DMA((N_REMOTE,)),
        pltpu.SemaphoreType.DMA((N_REMOTE,)),
        pltpu.SemaphoreType.DMA((N_LOCAL,)),
    ]
    anywhere = pl.BlockSpec(memory_space=pl.ANY)
    return pl.pallas_call(
        main_kernel,
        out_shape=(
            jax.ShapeDtypeStruct((1, ROWS), F32),
            jax.ShapeDtypeStruct((ROWS, E), F32),
            jax.ShapeDtypeStruct((SPAN, BLOCK), F32),
        ),
        in_specs=[anywhere] * 4,
        out_specs=(pl.BlockSpec(memory_space=pltpu.VMEM), anywhere, anywhere),
        scratch_shapes=scratch,
        compiler_params=pltpu.CompilerParams(
            collective_id=0, has_side_effects=True, vmem_limit_bytes=60 * 2**20
        ),
        name="distill",
    )(queries, passages, candidates, scores)


def finish_kernel(*refs):
    sources, sinks, stages, sems = refs[:3], refs[3:6], refs[6:9], refs[9]
    pieces = [(0, pl.ds(first, PIECE)) for first in range(0, ROWS, PIECE)]
    pieces += [(1, slice(None)), (2, slice(None))]
    loads, stores = [], []
    for index, (which, rows) in enumerate(pieces):
        source, stage, sink = sources[which], stages[which], sinks[which]
        loads.append(pltpu.make_async_copy(source.at[rows], stage.at[rows], sems.at[0, index]))
        stores.append(pltpu.make_async_copy(stage.at[rows], sink.at[rows], sems.at[1, index]))
    for copy in loads:
        copy.start()
    for load, store in zip(loads, stores):
        load.wait()
        store.start()
    for copy in stores:
        copy.wait()


def finish(*arrays):
    anywhere = pl.BlockSpec(memory_space=pl.ANY)
    return pl.pallas_call(
        finish_kernel,
        out_shape=tuple(jax.ShapeDtypeStruct(a.shape, a.dtype) for a in arrays),
        in_specs=[anywhere] * 3,
        out_specs=(anywhere,) * 3,
        scratch_shapes=[pltpu.VMEM(a.shape, a.dtype) for a in arrays]
        + [pltpu.SemaphoreType.DMA((2, ROWS // PIECE + 2))],
        compiler_params=pltpu.CompilerParams(vmem_limit_bytes=60 * 2**20),
        name="finish",
    )(*arrays)


def shards(queries, passages, candidates, teacher_scores):
    loss, grad_queries, grad_passages = main_call(queries, passages, candidates, teacher_scores)
    grad_queries, grad_passages, loss = finish(grad_queries, grad_passages, loss)
    return (loss.reshape(ROWS), grad_queries, grad_passages)


def solution(mesh):
    return jax.shard_map(
        shards,
        mesh=mesh,
        in_specs=(
            P(("query", "passage"), None),
            P("passage", None),
            P(("query", "passage"), None),
            P(("query", "passage"), None),
        ),
        out_specs=(P(("query", "passage")), P(("query", "passage"), None), P("passage", "query")),
        check_vma=False,
    )
```

```python
import functools
import math

import jax
import jax.numpy as jnp
from jax import lax
from jax.experimental import pallas as pl
from jax.experimental.pallas import tpu as pltpu
from jax.sharding import PartitionSpec as P

MESH = pl.DeviceIdType.MESH
BF16 = jnp.bfloat16
F32 = jnp.float32

E = 4096
W1, W2, W3 = 64, 256, 1024
WIDTHS = (W1, W2, W3, E)
ROWS = 128
SPAN = 32
HALF = 16
NX, NY, NZ = 4, 4, 8
POOL = 2 * NZ * SPAN
GROUP = NZ * SPAN
LANES = 128
BIG = 3.0e38
PIECE = 16
STRIP = 128

QUARTER = 384
FLAT = E - 4 * QUARTER
PIECES = 2
GATHER_ORDER = (
    ('m', 1), ('x', 0), (0, 1), (1, 1), ('m', 2), ('x', 1), (0, 2), (1, 2), ('m', 3), ('x', 2), (0, 3), (1, 3), ('m', 4), ('x', 3), (0, 4), (1, 4), ('x', 4)
)

BLOCK = 512
WA = 128
WB = BLOCK - WA
FIRST_Z = 2
CHUNKS = ((0, 5), (5, 3))
FAR = (3, 4, 5)


def place():
    query = lax.axis_index("query")
    passage = lax.axis_index("passage")
    x = (query // 4) * 2 + (passage // 2) % 2
    return x, query % 4, passage // 4, passage % 2


def device(x, y, z, core):
    x, y, z = x % NX, y % NY, z % NZ
    return ((x // 2) * 4 + y, (z * 2 + x % 2) * 2 + core)


SCRATCH = dict(
    qs=((2 * ROWS, E), BF16),
    ws=((2 * GROUP, E), BF16),
    cs=((2 * ROWS, LANES), jnp.int32),
    rs=((2 * ROWS, LANES), F32),
    ts=((2 * ROWS, LANES), F32),
    tt=((POOL, 2 * ROWS), F32),
    lv=((4, POOL, 2 * ROWS), F32),
    st=((2, 3, 8, ROWS), F32),
    sr=((2, 3, 8, ROWS), F32),
    grid=((4, POOL, 2 * ROWS), BF16),
    turned=((4, 2 * ROWS, POOL), BF16),
    go=((ROWS, E), F32),
    gs=((ROWS, E), F32),
    gr=((ROWS, E), F32),
    pa=((NZ, 2, 8, SPAN, WA), F32),
    pab=((NZ, 2, 8, SPAN, WA), BF16),
    ra=((2, 4, 2, 8, SPAN, WA), BF16),
    fa=((2, 2, 4, SPAN, WA), F32),
    rax=((3, 4, HALF, WA), F32),
    ga=((4, HALF, WA), F32),
    ray=((3, HALF, WA), F32),
    ray_low=((3, 2, 2, HALF, WA), F32),
    ga_low=((2, 2, HALF, WA), F32),
    rax_low=((3, HALF, WA), F32),
    pb=((2, 2, 4, NZ, HALF, WB), F32),
    pbb=((2, 2, 4, NZ, HALF, WB), BF16),
    rbr=((2, 2, NZ, HALF, WB), BF16),
    rbx=((2, 4, NZ, HALF, WB), BF16),
    gb=((4, NZ, HALF, WB), F32),
    gbb=((4, NZ, HALF, WB), BF16),
    rby=((3, NZ, HALF, WB), BF16),
    hb=((NZ, HALF, WB), F32),
    hbb=((NZ, HALF, WB), BF16),
    rbz=((NZ, HALF, WB), F32),
    rbzb=((NZ, HALF, WB), BF16),
    pc=((4, 2, 2, NZ, HALF, WB), F32),
    pcb=((4, 2, 2, NZ, HALF, WB), BF16),
    rcr=((2, 2, NZ, HALF, WB), BF16),
    rcy=((2, 2, 2, NZ, HALF, WB), BF16),
    gc=((2, 2, NZ, HALF, WB), F32),
    gcb=((2, 2, NZ, HALF, WB), BF16),
    rcx=((3, NZ, HALF, WB), BF16),
    hc=((NZ, HALF, WB), F32),
    hcb=((NZ, HALF, WB), BF16),
    rcz=((NZ, HALF, WB), F32),
    rczb=((NZ, HALF, WB), BF16),
    ob=((SPAN, BLOCK), F32),
)
N_REMOTE = 260
N_LOCAL = 16


def main_kernel(queries, passages, candidates, scores, loss, grad_queries, grad_passages, *scratch):
    buf = dict(zip(SCRATCH, scratch))
    send_sems, recv_sems, local_sems = scratch[len(SCRATCH) :]
    qs, ws, tt, lv, st, sr, grid = (buf[k] for k in ("qs", "ws", "tt", "lv", "st", "sr", "grid"))
    go, gs, gr = (buf[k] for k in ("go", "gs", "gr"))
    x, y, z, core = place()
    xh = x // 2
    used = [0, 0]
    sent = []

    def remote(src, dst, target):
        index = used[0]
        used[0] += 1
        copy = pltpu.make_async_remote_copy(
            src_ref=src,
            dst_ref=dst,
            send_sem=send_sems.at[index],
            recv_sem=recv_sems.at[index],
            device_id=target,
            device_id_type=MESH,
        )
        copy.start()
        sent.append(copy)
        return copy

    def local(src, dst):
        index = used[1]
        used[1] += 1
        copy = pltpu.make_async_copy(src, dst, local_sems.at[index])
        copy.start()
        return copy

    sibling = device(x, y, z, 1 - core)
    by_x = {d: device(x + d, y, z, core) for d in (1, 2, 3)}
    by_y = {d: device(x, y + d, z, core) for d in (1, 2, 3)}
    by_z = {d: device(x, y, z + d, core) for d in range(1, NZ)}
    peers = [sibling, *by_x.values(), *by_y.values(), by_z[1], by_z[NZ - 1]]

    own_block = local(passages, ws.at[pl.ds(0, SPAN)])
    own_queries = local(queries, qs.at[pl.ds(0, ROWS)])
    own_teacher = [
        local(candidates, buf["cs"].at[pl.ds(0, ROWS)]),
        local(scores, buf["rs"].at[pl.ds(0, ROWS)]),
    ]
    barrier = pltpu.get_barrier_semaphore()
    for peer in peers:
        pl.semaphore_signal(barrier, inc=1, device_id=peer, device_id_type=MESH)
    pl.semaphore_wait(barrier, len(peers))

    mine = pl.ds(pl.multiple_of(FLAT + QUARTER * y, LANES), QUARTER)
    pieces = {"m": mine}
    for index in range(PIECES):
        pieces[index] = pl.ds(index * (FLAT // PIECES), FLAT // PIECES)

    def row(dxl, dz):
        return dxl * GROUP + (dz % NZ) * SPAN

    z_copies, x_copies, y_copies = {}, {}, ([], [])

    def along_z(piece, step, way):
        dz, cols = -way * step, pieces[piece]
        first, count = (0 if way > 0 else HALF, HALF) if step == 3 else (0, SPAN)
        here = pl.ds(row(0, dz) + first, count)
        there = pl.ds(row(0, dz - way) + first, count)
        target = by_z[1 if way > 0 else NZ - 1]
        z_copies[piece, step + 1, way] = remote(ws.at[here, cols], ws.at[there, cols], target)

    def along_x(piece, dz):
        cols = pieces[piece]
        copies = []
        for d, first in ((1, 0), (3, HALF)):
            here = pl.ds(row(0, dz) + first, HALF)
            there = pl.ds(row(1, dz) + first, HALF)
            copies.append(remote(ws.at[here, cols], ws.at[there, cols], by_x[d]))
        x_copies[piece, dz] = copies

    def along_y(dxl, dz):
        here = ws.at[pl.ds(row(dxl, dz), SPAN), mine]
        for d in (2, 1, 3):
            y_copies[dxl].append(remote(here, here, by_y[d]))

    def arrived_here(copies):
        for copy in copies:
            copy.wait()

    def arrived(copies):
        for copy in copies:
            copy.wait_recv()

    own_block.wait()
    for piece in ('m', 0, 1):
        for way in (1, -1):
            along_z(piece, 0, way)
        along_x(piece, 0)
    to_sibling = [
        remote(candidates, buf["cs"].at[pl.ds(ROWS, ROWS)], sibling),
        remote(scores, buf["rs"].at[pl.ds(ROWS, ROWS)], sibling),
        remote(queries, qs.at[pl.ds(ROWS, ROWS)], sibling),
    ]
    x_done = set()

    def from_x(piece, dz):
        arrived(x_copies[piece, dz])
        x_done.add((piece, dz))
        if piece == "m":
            along_y(1, dz)

    cs, rs, ts = buf["cs"], buf["rs"], buf["ts"]
    lane = lax.broadcasted_iota(jnp.int32, (ROWS, LANES), 1)
    entropy = []

    def teach(rows):
        raw = rs[rows]
        shifted = raw - jnp.max(raw, axis=1, keepdims=True)
        log_teacher = shifted - jnp.log(jnp.sum(jnp.exp(shifted), axis=1, keepdims=True))
        value = jnp.exp(log_teacher)
        ts[rows] = value
        entropy.append(jnp.sum(value * log_teacher, axis=1, keepdims=True))

    def spread(rows, chunk):
        chosen = cs[rows]
        slot = lane // SPAN + chunk * (LANES // SPAN)
        dxl, dz = slot // NZ, slot % NZ
        owner = (((z + dz) % NZ) * 2 + (x + dxl) % 2) * 2 + core
        target = owner * SPAN + lane % SPAN
        position = jnp.zeros((ROWS, LANES), jnp.int32)
        for step in (64, 32, 16, 8, 4, 2, 1):
            probe = jnp.take_along_axis(chosen, position + (step - 1), axis=1)
            position = jnp.where(probe < target, position + step, position)
        hit = jnp.take_along_axis(chosen, position, axis=1) == target
        value = jnp.take_along_axis(ts[rows], position, axis=1)
        tt[chunk * LANES : (chunk + 1) * LANES, rows] = jnp.where(hit, value, -1.0).T

    own, other = pl.ds(0, ROWS), pl.ds(ROWS, ROWS)
    chores = [lambda: (arrived_here(own_teacher), teach(own))]
    chores += [lambda chunk=chunk: spread(own, chunk) for chunk in range(POOL // LANES)]
    chores += [lambda: (arrived(to_sibling[:2]), teach(other))]
    chores += [lambda chunk=chunk: spread(other, chunk) for chunk in range(POOL // LANES)]

    for piece, step in GATHER_ORDER:
        if piece == "x":
            for dz in ((0,) if step == 0 else (4,) if step == 4 else (-step, step)):
                from_x("m", dz)
            continue
        for way in (1, -1):
            z_copies[piece, step, way].wait_recv()
            if step < 4:
                along_x(piece, -way * step)
                along_z(piece, step, way)
                if piece == "m":
                    along_y(0, -way * step)
        if step == 4:
            along_x(piece, 4)
            if piece == "m":
                along_y(0, 4)
        if chores and (piece, step) != ("m", 1):
            chores.pop(0)()
    for chore in chores:
        chore()
    def dot_rows(a, b):
        return lax.dot_general(a, b, (((1,), (1,)), ((), ())), preferred_element_type=F32)

    column = lax.broadcasted_iota(jnp.int32, (2 * ROWS, W2), 1)
    own_queries.wait()
    arrived(to_sibling[2:])
    for dxl in range(2):
        if dxl == 1:
            for key in x_copies:
                if key not in x_done:
                    from_x(*key)
        arrived(y_copies[dxl])
        rows = pl.ds(dxl * GROUP, GROUP)
        head = qs[:, 0:W2]
        zero = jnp.zeros_like(head)
        narrow = ws[rows, 0:W2]
        level = dot_rows(narrow, jnp.where(column < W1, head, zero))
        lv[0, rows] = level
        level += dot_rows(narrow, jnp.where(column < W1, zero, head))
        lv[1, rows] = level
        level += dot_rows(ws[rows, W2:W3], qs[:, W2:W3])
        lv[2, rows] = level

        def score_step(index, total, rows=rows):
            cols = pl.ds(pl.multiple_of(index * 1024, 1024), 1024)
            return total + dot_rows(ws[rows, cols], qs[:, cols])

        lv[3, rows] = lax.fori_loop(1, E // 1024, score_step, level)


    scales = [1.0 / math.sqrt(width) for width in WIDTHS]
    strips = [pl.ds(first, STRIP) for first in range(0, POOL, STRIP)]

    def tabulate(rows):
        rows = rows + [jnp.zeros((1, ROWS), F32)] * (8 - len(rows))
        return jnp.concatenate(rows, axis=0)

    def gather_terms(half):
        lanes = pl.ds(half * ROWS, ROWS)
        tops, sums, parts = [], [], []
        weight_sum = jnp.zeros((1, ROWS), F32)
        for strip in strips:
            weight_sum += jnp.sum(jnp.maximum(tt[strip, lanes], 0.0), axis=0, keepdims=True)
        for level in range(4):
            top = jnp.full((1, ROWS), -BIG, F32)
            for strip in strips:
                logits = jnp.where(
                    tt[strip, lanes] >= 0.0, lv[level, strip, lanes] * scales[level], -BIG
                )
                lv[level, strip, lanes] = logits
                top = jnp.maximum(top, jnp.max(logits, axis=0, keepdims=True))
            total = jnp.zeros((1, ROWS), F32)
            part = jnp.zeros((1, ROWS), F32)
            for strip in strips:
                shifted = lv[level, strip, lanes] - top
                weight = jnp.exp(shifted)
                lv[level, strip, lanes] = weight
                total += jnp.sum(weight, axis=0, keepdims=True)
                teacher = jnp.maximum(tt[strip, lanes], 0.0)
                part += jnp.sum(teacher * shifted, axis=0, keepdims=True)
            tops.append(top)
            sums.append(total)
            parts.append(part)
        st[half, 0] = tabulate(tops)
        st[half, 1] = tabulate(sums)
        st[half, 2] = tabulate(parts + [weight_sum])

    stats_copies = []
    for half in range(2):
        gather_terms(half)
        stats_copies.append(remote(st.at[half], sr.at[1 - half], sibling))

    loss_terms = []

    def finish_terms(half):
        lanes = pl.ds(half * ROWS, ROWS)
        top, top_other = st[half, 0], sr[half, 0]
        peak = jnp.maximum(top, top_other)
        fade, fade_other = jnp.exp(top - peak), jnp.exp(top_other - peak)
        total = st[half, 1] * fade + sr[half, 1] * fade_other
        factor = fade / total
        if half == 0:
            part, part_other = st[half, 2], sr[half, 2]
            weight, weight_other = part[4:5], part_other[4:5]
            part = part + weight * (top - peak) + part_other + weight_other * (top_other - peak)
            terms = jnp.log(total) * (weight + weight_other) - part
            loss_terms.append(jnp.sum(terms[:4], axis=0, keepdims=True))
        for strip in strips:
            teacher = jnp.maximum(tt[strip, lanes], 0.0)
            tail = None
            for level in (3, 2, 1, 0):
                student = lv[level, strip, lanes] * factor[level : level + 1]
                dlogit = (student - teacher) * scales[level]
                tail = dlogit if tail is None else dlogit + tail
                grid[level, strip, lanes] = tail.astype(BF16)

    for half in (1, 0):
        stats_copies[1 - half].wait_recv()
        finish_terms(half)


    pa, pab, pb, pbb, pc, pcb = (buf[k] for k in ("pa", "pab", "pb", "pbb", "pc", "pcb"))

    def dot_plain(a, b):
        return jnp.dot(a, b, preferred_element_type=F32)

    def keep(dxl, q, result):
        rounded = result.astype(BF16)
        xh_of, y_of = q // 4, q % 4
        for dz in range(NZ):
            top = slice(dz * SPAN, dz * SPAN + HALF)
            low = slice(dz * SPAN + HALF, (dz + 1) * SPAN)
            whole = slice(dz * SPAN, (dz + 1) * SPAN)
            pa[dz, dxl, q] = result[whole, :WA]
            pab[dz, dxl, q] = rounded[whole, :WA]
            at = (dz - FIRST_Z) % NZ
            pb[dxl, xh_of, y_of, at] = result[top, WA:]
            pbb[dxl, xh_of, y_of, at] = rounded[top, WA:]
            pc[y_of, dxl, xh_of, at] = result[low, WA:]
            pcb[y_of, dxl, xh_of, at] = rounded[low, WA:]

    ra, rax, ray, fa, ga = (buf[k] for k in ("ra", "rax", "ray", "fa", "ga"))
    ray_low, ga_low, rax_low = (buf[k] for k in ("ray_low", "ga_low", "rax_low"))

    def ring(way, step, dxl):
        dz = (way * (5 - step)) % NZ
        target = by_z[1 if way > 0 else NZ - 1]
        slot = ra.at[0 if way > 0 else 1, step - 1, dxl]
        if step == 1:
            rows = pl.ds(0 if way > 0 else HALF, HALF)
            return remote(pab.at[dz, dxl, :, rows], slot.at[:, rows], target)
        return remote(pab.at[dz, dxl], slot, target)

    def toward(d):
        return ((x + d) % NX) // 2

    rings = {}
    gb, gbb, rbx, rby = (buf[k] for k in ("gb", "gbb", "rbx", "rby"))
    gc, gcb, rcy, rcx = (buf[k] for k in ("gc", "gcb", "rcy", "rcx"))
    rbr, rcr = buf["rbr"], buf["rcr"]
    b_far, c_far, b_copies, c_copies = [], [], [[], []], [[], []]

    def opposite_b(chunk):
        part = pl.ds(*CHUNKS[chunk])
        b_far.append(
            [
                remote(pbb.at[0, toward(2), pl.ds(2 * h, 2), part], rbr.at[h, :, part], by_x[d])
                for h, d in ((0, 1), (1, 3))
            ]
        )

    def opposite_c(chunk):
        part = pl.ds(*CHUNKS[chunk])
        c_far.append(
            [
                remote(pcb.at[(y + 2) % NY, h, :, part], rcr.at[h, :, part], by_y[d])
                for h, d in ((0, 1), (1, 3))
            ]
        )

    def direct(chunk):
        part = pl.ds(*CHUNKS[chunk])
        for h, d in ((1, 1), (0, 3)):
            b_copies[chunk].append(
                remote(
                    pbb.at[1, toward(d), pl.ds(2 * h, 2), part],
                    rbx.at[1 - h, pl.ds(2 * h, 2), part],
                    by_x[d],
                )
            )
            c_copies[chunk].append(
                remote(pcb.at[(y + d) % NY, h, :, part], rcy.at[1 - h, h, :, part], by_y[d])
            )

    def relay(chunk):
        part = pl.ds(*CHUNKS[chunk])
        arrived(b_far[chunk])
        for h, d in ((0, 1), (1, 3)):
            half = pl.ds(2 * h, 2)
            total = pb[1, toward(d), half, part] + rbr[h, :, part].astype(F32)
            pbb[1, toward(d), half, part] = total.astype(BF16)
            b_copies[chunk].append(
                remote(pbb.at[1, toward(d), half, part], rbx.at[h, half, part], by_x[d])
            )
        arrived(c_far[chunk])
        for h, d in ((0, 1), (1, 3)):
            to = (y + d) % NY
            total = pc[to, h, :, part] + rcr[h, :, part].astype(F32)
            pcb[to, h, :, part] = total.astype(BF16)
            c_copies[chunk].append(
                remote(pcb.at[to, h, :, part], rcy.at[h, h, :, part], by_y[d])
            )

    for dxl in range(2):
        part = pl.ds(dxl * GROUP, GROUP)
        narrow = lax.broadcasted_iota(jnp.int32, (GROUP, W2), 1) < W1
        first = qs[:, 0:W2]
        first = jnp.where(
            narrow, dot_plain(grid[0, part], first), dot_plain(grid[1, part], first)
        )
        second = dot_plain(grid[2, part], qs[:, W2:BLOCK])
        keep(dxl, 0, jnp.concatenate([first, second], axis=1))
        keep(dxl, 1, dot_plain(grid[2, part], qs[:, BLOCK : 2 * BLOCK]))
        for q in range(2, 8):
            keep(dxl, q, dot_plain(grid[3, part], qs[:, q * BLOCK : (q + 1) * BLOCK]))
        for way in (1, -1):
            rings[way, dxl] = ring(way, 1, dxl)
        if dxl == 0:
            opposite_b(0)
    opposite_c(0)
    direct(0)

    diagonal = lax.broadcasted_iota(jnp.int32, (ROWS, LANES), 0) == lax.broadcasted_iota(
        jnp.int32, (ROWS, LANES), 1
    )
    entropy_row = jnp.sum(jnp.where(diagonal, entropy[0], 0.0), axis=0, keepdims=True)
    loss[...] = 4.0 * entropy_row + loss_terms[0]

    turned = buf["turned"]
    for level in range(4):
        turned[level] = grid[level].T

    def keep_query(cols, result):
        go[:, cols] = result[:ROWS]
        gs[:, cols] = result[ROWS:]

    first = ws[:, 0:W2]
    keep_query(
        slice(0, W2), jnp.where(column < W1, dot_plain(turned[0], first), dot_plain(turned[1], first))
    )
    keep_query(slice(W2, BLOCK), dot_plain(turned[2], ws[:, W2:BLOCK]))
    keep_query(slice(BLOCK, W3), dot_plain(turned[2], ws[:, BLOCK:W3]))

    def query_step(index, carry):
        cols = pl.ds(pl.multiple_of(index * BLOCK, BLOCK), BLOCK)
        keep_query(cols, dot_plain(turned[3], ws[:, cols]))
        return carry


    def ring_step(step):
        for dxl in range(2):
            for way in (1, -1):
                rings[way, dxl].wait_recv()
                dz = (way * (4 - step)) % NZ
                slot = ra.at[0 if way > 0 else 1, step - 1, dxl]
                rows = pl.ds(0, SPAN)
                if step == 1:
                    rows = pl.ds(0 if way > 0 else HALF, HALF)
                pab[dz, dxl, :, rows] = (pa[dz, dxl, :, rows] + slot[:, rows].astype(F32)).astype(
                    BF16
                )
                rings[way, dxl] = ring(way, step + 1, dxl)

    def ring_end():
        for dxl in range(2):
            rings[1, dxl].wait_recv()
            rings[-1, dxl].wait_recv()
            total = pa[0, dxl] + ra[0, 3, dxl].astype(F32) + ra[1, 3, dxl].astype(F32)
            fa[dxl] = total.reshape(2, 4, SPAN, WA)
        top, low = pl.ds(0, HALF), pl.ds(HALF, HALF)
        return (
            [remote(fa.at[d % 2, toward(d), :, top], rax.at[d - 1], by_x[d]) for d in (2, 1, 3)],
            [
                remote(fa.at[:, :, (y + d) % NY, low], ray_low.at[d - 1], by_y[d])
                for d in (2, 1, 3)
            ],
        )

    def three(own, parts):
        return own + parts[0].astype(F32) + parts[1].astype(F32) + parts[2].astype(F32)

    def b_second(chunk):
        part = pl.ds(*CHUNKS[chunk])
        arrived(b_copies[chunk])
        total = pb[0, xh, :, part] + rbx[0, :, part].astype(F32) + rbx[1, :, part].astype(F32)
        gb[:, part] = total
        gbb[:, part] = total.astype(BF16)
        return [
            remote(gbb.at[(y + d) % NY, part], rby.at[d - 1, part], by_y[d]) for d in (2, 1, 3)
        ]

    def c_second(chunk):
        part = pl.ds(*CHUNKS[chunk])
        arrived(c_copies[chunk])
        total = pc[y, :, :, part] + rcy[0, :, :, part].astype(F32)
        total += rcy[1, :, :, part].astype(F32)
        gc[:, :, part] = total
        gcb[:, :, part] = total.astype(BF16)
        return [
            remote(gcb.at[d % 2, toward(d), part], rcx.at[d - 1, part], by_x[d]) for d in (2, 1, 3)
        ]

    def third(chunk, total, wide, narrow, wide_in, narrow_in):
        start, count = CHUNKS[chunk]
        wide[pl.ds(start, count)] = total
        narrow[pl.ds(start, count)] = total.astype(BF16)
        copies = []
        for at in range(start, start + count):
            dz = (at + FIRST_Z) % NZ
            if dz in FAR:
                copies.append(remote(narrow.at[at], narrow_in.at[at], by_z[dz]))
            elif dz:
                copies.append(remote(wide.at[at], wide_in.at[at], by_z[dz]))
        return copies

    hb, hbb, rbz, rbzb = (buf[k] for k in ("hb", "hbb", "rbz", "rbzb"))
    hc, hcb, rcz, rczb = (buf[k] for k in ("hc", "hcb", "rcz", "rczb"))

    def b_third(chunk):
        part = pl.ds(*CHUNKS[chunk])
        arrived(b_next[chunk])
        return third(chunk, three(gb[y, part], rby[:, part]), hb, hbb, rbz, rbzb)

    def c_third(chunk):
        part = pl.ds(*CHUNKS[chunk])
        arrived(c_next[chunk])
        return third(chunk, three(gc[0, xh, part], rcx[:, part]), hc, hcb, rcz, rczb)

    b_next, c_next, last_copies = [None, None], [None, None], []
    relay(0)
    opposite_b(1)
    opposite_c(1)
    direct(1)
    ring_step(1)
    ring_step(2)
    lax.fori_loop(2, E // BLOCK, query_step, 0)
    query_copy = remote(gs, gr, sibling)
    b_next[0] = b_second(0)
    c_next[0] = c_second(0)
    ring_step(3)
    relay(1)
    last_copies += b_third(0)
    last_copies += c_third(0)
    a_copies = ring_end()
    b_next[1] = b_second(1)
    c_next[1] = c_second(1)
    arrived(a_copies[0])
    ga[...] = three(fa[0, xh, :, :HALF], rax)
    a_last = [remote(ga.at[(y + d) % NY], ray.at[d - 1], by_y[d]) for d in (2, 1, 3)]
    arrived(a_copies[1])
    ga_low[...] = three(fa[:, :, y, HALF:], ray_low)
    a_last += [
        remote(ga_low.at[d % 2, toward(d)], rax_low.at[d - 1], by_x[d]) for d in (2, 1, 3)
    ]
    last_copies += b_third(1)
    last_copies += c_third(1)
    query_copy.wait_recv()
    go[...] += gr[...]
    out_copy = local(go, grad_queries)
    arrived(a_last)
    ob = buf["ob"]
    ob[:HALF, :WA] = three(ga[y], ray)
    ob[HALF:, :WA] = three(ga_low[0, xh], rax_low)
    arrived(last_copies)
    at_home = (0 - FIRST_Z) % NZ
    total_b, total_c = hb[at_home], hc[at_home]
    for at in range(NZ):
        if (at + FIRST_Z) % NZ in FAR:
            total_b += rbzb[at].astype(F32)
            total_c += rczb[at].astype(F32)
        elif at != at_home:
            total_b += rbz[at]
            total_c += rcz[at]
    ob[:HALF, WA:] = total_b
    ob[HALF:, WA:] = total_c
    last = local(ob, grad_passages)
    for copy in sent:
        copy.wait_send()
    out_copy.wait()
    last.wait()


def main_call(queries, passages, candidates, scores):
    scratch = [pltpu.VMEM(shape, dtype) for shape, dtype in SCRATCH.values()]
    scratch += [
        pltpu.SemaphoreType.DMA((N_REMOTE,)),
        pltpu.SemaphoreType.DMA((N_REMOTE,)),
        pltpu.SemaphoreType.DMA((N_LOCAL,)),
    ]
    anywhere = pl.BlockSpec(memory_space=pl.ANY)
    return pl.pallas_call(
        main_kernel,
        out_shape=(
            jax.ShapeDtypeStruct((1, ROWS), F32),
            jax.ShapeDtypeStruct((ROWS, E), F32),
            jax.ShapeDtypeStruct((SPAN, BLOCK), F32),
        ),
        in_specs=[anywhere] * 4,
        out_specs=(pl.BlockSpec(memory_space=pltpu.VMEM), anywhere, anywhere),
        scratch_shapes=scratch,
        compiler_params=pltpu.CompilerParams(
            collective_id=0, has_side_effects=True, vmem_limit_bytes=60 * 2**20
        ),
        name="distill",
    )(queries, passages, candidates, scores)


def finish_kernel(*refs):
    sources, sinks, stages, sems = refs[:3], refs[3:6], refs[6:9], refs[9]
    pieces = [(0, pl.ds(first, PIECE)) for first in range(0, ROWS, PIECE)]
    pieces += [(1, slice(None)), (2, slice(None))]
    loads, stores = [], []
    for index, (which, rows) in enumerate(pieces):
        source, stage, sink = sources[which], stages[which], sinks[which]
        loads.append(pltpu.make_async_copy(source.at[rows], stage.at[rows], sems.at[0, index]))
        stores.append(pltpu.make_async_copy(stage.at[rows], sink.at[rows], sems.at[1, index]))
    for copy in loads:
        copy.start()
    for load, store in zip(loads, stores):
        load.wait()
        store.start()
    for copy in stores:
        copy.wait()


def finish(*arrays):
    anywhere = pl.BlockSpec(memory_space=pl.ANY)
    return pl.pallas_call(
        finish_kernel,
        out_shape=tuple(jax.ShapeDtypeStruct(a.shape, a.dtype) for a in arrays),
        in_specs=[anywhere] * 3,
        out_specs=(anywhere,) * 3,
        scratch_shapes=[pltpu.VMEM(a.shape, a.dtype) for a in arrays]
        + [pltpu.SemaphoreType.DMA((2, ROWS // PIECE + 2))],
        compiler_params=pltpu.CompilerParams(vmem_limit_bytes=60 * 2**20),
        name="finish",
    )(*arrays)


def shards(queries, passages, candidates, teacher_scores):
    loss, grad_queries, grad_passages = main_call(queries, passages, candidates, teacher_scores)
    grad_queries, grad_passages, loss = finish(grad_queries, grad_passages, loss)
    return (loss.reshape(ROWS), grad_queries, grad_passages)


def solution(mesh):
    return jax.shard_map(
        shards,
        mesh=mesh,
        in_specs=(
            P(("query", "passage"), None),
            P("passage", None),
            P(("query", "passage"), None),
            P(("query", "passage"), None),
        ),
        out_specs=(P(("query", "passage")), P(("query", "passage"), None), P("passage", "query")),
        check_vma=False,
    )
```

```python
import functools
import math

import jax
import jax.numpy as jnp
from jax import lax
from jax.experimental import pallas as pl
from jax.experimental.pallas import tpu as pltpu
from jax.sharding import PartitionSpec as P

MESH = pl.DeviceIdType.MESH
BF16 = jnp.bfloat16
F32 = jnp.float32

E = 4096
W1, W2, W3 = 64, 256, 1024
WIDTHS = (W1, W2, W3, E)
ROWS = 128
SPAN = 32
HALF = 16
NX, NY, NZ = 4, 4, 8
POOL = 2 * NZ * SPAN
GROUP = NZ * SPAN
LANES = 128
BIG = 3.0e38
PIECE = 16
STRIP = 128

QUARTER = 384
FLAT = E - 4 * QUARTER
PIECES = 2
GATHER_ORDER = (
    ('m', 1), ('x', 0), (0, 1), (1, 1), ('m', 2), ('x', 1), (0, 2), (1, 2), ('m', 3), ('x', 2), (0, 3), (1, 3), ('m', 4), ('x', 3), (0, 4), (1, 4), ('x', 4)
)

BLOCK = 512
WA = 128
WB = BLOCK - WA
FIRST_Z = 2
CHUNKS = ((0, 5), (5, 3))
FAR = (3, 4, 5)


def place():
    query = lax.axis_index("query")
    passage = lax.axis_index("passage")
    x = (query // 4) * 2 + (passage // 2) % 2
    return x, query % 4, passage // 4, passage % 2


def device(x, y, z, core):
    x, y, z = x % NX, y % NY, z % NZ
    return ((x // 2) * 4 + y, (z * 2 + x % 2) * 2 + core)


SCRATCH = dict(
    qs=((2 * ROWS, E), BF16),
    ws=((2 * GROUP, E), BF16),
    cs=((2 * ROWS, LANES), jnp.int32),
    rs=((2 * ROWS, LANES), F32),
    ts=((2 * ROWS, LANES), F32),
    tt=((POOL, 2 * ROWS), F32),
    lv=((4, POOL, 2 * ROWS), F32),
    st=((2, 3, 8, ROWS), F32),
    sr=((2, 3, 8, ROWS), F32),
    grid=((4, POOL, 2 * ROWS), BF16),
    turned=((4, 2 * ROWS, POOL), BF16),
    go=((ROWS, E), F32),
    gs=((ROWS, E), F32),
    gr=((ROWS, E), F32),
    pa=((NZ, 2, 8, SPAN, WA), F32),
    pab=((NZ, 2, 8, SPAN, WA), BF16),
    ra=((2, 4, 2, 8, SPAN, WA), BF16),
    fa=((2, 2, 4, SPAN, WA), F32),
    rax=((3, 4, HALF, WA), F32),
    ga=((4, HALF, WA), F32),
    ray=((3, HALF, WA), F32),
    ray_low=((3, 2, 2, HALF, WA), F32),
    ga_low=((2, 2, HALF, WA), F32),
    rax_low=((3, HALF, WA), F32),
    pb=((2, 2, 4, NZ, HALF, WB), F32),
    pbb=((2, 2, 4, NZ, HALF, WB), BF16),
    rbr=((2, 2, NZ, HALF, WB), BF16),
    rbx=((2, 4, NZ, HALF, WB), BF16),
    gb=((4, NZ, HALF, WB), F32),
    gbb=((4, NZ, HALF, WB), BF16),
    rby=((3, NZ, HALF, WB), BF16),
    hb=((NZ, HALF, WB), F32),
    hbb=((NZ, HALF, WB), BF16),
    rbz=((NZ, HALF, WB), F32),
    rbzb=((NZ, HALF, WB), BF16),
    pc=((4, 2, 2, NZ, HALF, WB), F32),
    pcb=((4, 2, 2, NZ, HALF, WB), BF16),
    rcr=((2, 2, NZ, HALF, WB), BF16),
    rcy=((2, 2, 2, NZ, HALF, WB), BF16),
    gc=((2, 2, NZ, HALF, WB), F32),
    gcb=((2, 2, NZ, HALF, WB), BF16),
    rcx=((3, NZ, HALF, WB), BF16),
    hc=((NZ, HALF, WB), F32),
    hcb=((NZ, HALF, WB), BF16),
    rcz=((NZ, HALF, WB), F32),
    rczb=((NZ, HALF, WB), BF16),
    ob=((SPAN, BLOCK), F32),
)
N_REMOTE = 260
N_LOCAL = 16


def main_kernel(queries, passages, candidates, scores, loss, grad_queries, grad_passages, *scratch):
    buf = dict(zip(SCRATCH, scratch))
    send_sems, recv_sems, local_sems = scratch[len(SCRATCH) :]
    qs, ws, tt, lv, st, sr, grid = (buf[k] for k in ("qs", "ws", "tt", "lv", "st", "sr", "grid"))
    go, gs, gr = (buf[k] for k in ("go", "gs", "gr"))
    x, y, z, core = place()
    xh = x // 2
    used = [0, 0]
    sent = []

    def remote(src, dst, target):
        index = used[0]
        used[0] += 1
        copy = pltpu.make_async_remote_copy(
            src_ref=src,
            dst_ref=dst,
            send_sem=send_sems.at[index],
            recv_sem=recv_sems.at[index],
            device_id=target,
            device_id_type=MESH,
        )
        copy.start()
        sent.append(copy)
        return copy

    def local(src, dst):
        index = used[1]
        used[1] += 1
        copy = pltpu.make_async_copy(src, dst, local_sems.at[index])
        copy.start()
        return copy

    sibling = device(x, y, z, 1 - core)
    by_x = {d: device(x + d, y, z, core) for d in (1, 2, 3)}
    by_y = {d: device(x, y + d, z, core) for d in (1, 2, 3)}
    by_z = {d: device(x, y, z + d, core) for d in range(1, NZ)}
    peers = [sibling, *by_x.values(), *by_y.values(), by_z[1], by_z[NZ - 1]]

    own_block = local(passages, ws.at[pl.ds(0, SPAN)])
    own_queries = local(queries, qs.at[pl.ds(0, ROWS)])
    own_teacher = [
        local(candidates, buf["cs"].at[pl.ds(0, ROWS)]),
        local(scores, buf["rs"].at[pl.ds(0, ROWS)]),
    ]
    barrier = pltpu.get_barrier_semaphore()
    for peer in peers:
        pl.semaphore_signal(barrier, inc=1, device_id=peer, device_id_type=MESH)
    pl.semaphore_wait(barrier, len(peers))

    mine = pl.ds(pl.multiple_of(FLAT + QUARTER * y, LANES), QUARTER)
    pieces = {"m": mine}
    for index in range(PIECES):
        pieces[index] = pl.ds(index * (FLAT // PIECES), FLAT // PIECES)

    def row(dxl, dz):
        return dxl * GROUP + (dz % NZ) * SPAN

    z_copies, x_copies, y_copies = {}, {}, ([], [])

    def along_z(piece, step, way):
        dz, cols = -way * step, pieces[piece]
        first, count = (0 if way > 0 else HALF, HALF) if step == 3 else (0, SPAN)
        here = pl.ds(row(0, dz) + first, count)
        there = pl.ds(row(0, dz - way) + first, count)
        target = by_z[1 if way > 0 else NZ - 1]
        z_copies[piece, step + 1, way] = remote(ws.at[here, cols], ws.at[there, cols], target)

    def along_x(piece, dz):
        cols = pieces[piece]
        copies = []
        for d, first in ((1, 0), (3, HALF)):
            here = pl.ds(row(0, dz) + first, HALF)
            there = pl.ds(row(1, dz) + first, HALF)
            copies.append(remote(ws.at[here, cols], ws.at[there, cols], by_x[d]))
        x_copies[piece, dz] = copies

    def along_y(dxl, dz):
        here = ws.at[pl.ds(row(dxl, dz), SPAN), mine]
        for d in (2, 1, 3):
            y_copies[dxl].append(remote(here, here, by_y[d]))

    def arrived_here(copies):
        for copy in copies:
            copy.wait()

    def arrived(copies):
        for copy in copies:
            copy.wait_recv()

    own_block.wait()
    for piece in ('m', 0, 1):
        for way in (1, -1):
            along_z(piece, 0, way)
        along_x(piece, 0)
    to_sibling = [
        remote(candidates, buf["cs"].at[pl.ds(ROWS, ROWS)], sibling),
        remote(scores, buf["rs"].at[pl.ds(ROWS, ROWS)], sibling),
        remote(queries, qs.at[pl.ds(ROWS, ROWS)], sibling),
    ]
    x_done = set()

    def from_x(piece, dz):
        arrived(x_copies[piece, dz])
        x_done.add((piece, dz))
        if piece == "m":
            along_y(1, dz)

    cs, rs, ts = buf["cs"], buf["rs"], buf["ts"]
    lane = lax.broadcasted_iota(jnp.int32, (ROWS, LANES), 1)
    entropy = []

    def teach(rows):
        raw = rs[rows]
        shifted = raw - jnp.max(raw, axis=1, keepdims=True)
        log_teacher = shifted - jnp.log(jnp.sum(jnp.exp(shifted), axis=1, keepdims=True))
        value = jnp.exp(log_teacher)
        ts[rows] = value
        entropy.append(jnp.sum(value * log_teacher, axis=1, keepdims=True))

    def spread(rows, chunk):
        chosen = cs[rows]
        slot = lane // SPAN + chunk * (LANES // SPAN)
        dxl, dz = slot // NZ, slot % NZ
        owner = (((z + dz) % NZ) * 2 + (x + dxl) % 2) * 2 + core
        target = owner * SPAN + lane % SPAN
        position = jnp.zeros((ROWS, LANES), jnp.int32)
        for step in (64, 32, 16, 8, 4, 2, 1):
            probe = jnp.take_along_axis(chosen, position + (step - 1), axis=1)
            position = jnp.where(probe < target, position + step, position)
        hit = jnp.take_along_axis(chosen, position, axis=1) == target
        value = jnp.take_along_axis(ts[rows], position, axis=1)
        tt[chunk * LANES : (chunk + 1) * LANES, rows] = jnp.where(hit, value, -1.0).T

    own, other = pl.ds(0, ROWS), pl.ds(ROWS, ROWS)
    chores = [lambda: (arrived_here(own_teacher), teach(own))]
    chores += [lambda chunk=chunk: spread(own, chunk) for chunk in range(POOL // LANES)]
    chores += [lambda: (arrived(to_sibling[:2]), teach(other))]
    chores += [lambda chunk=chunk: spread(other, chunk) for chunk in range(POOL // LANES)]

    for piece, step in GATHER_ORDER:
        if piece == "x":
            for dz in ((0,) if step == 0 else (4,) if step == 4 else (-step, step)):
                from_x("m", dz)
            continue
        for way in (1, -1):
            z_copies[piece, step, way].wait_recv()
            if step < 4:
                along_x(piece, -way * step)
                along_z(piece, step, way)
                if piece == "m":
                    along_y(0, -way * step)
        if step == 4:
            along_x(piece, 4)
            if piece == "m":
                along_y(0, 4)
        if chores and (piece, step) != ("m", 1):
            chores.pop(0)()
    for chore in chores:
        chore()
    def dot_rows(a, b):
        return lax.dot_general(a, b, (((1,), (1,)), ((), ())), preferred_element_type=F32)

    column = lax.broadcasted_iota(jnp.int32, (2 * ROWS, W2), 1)
    own_queries.wait()
    arrived(to_sibling[2:])
    for dxl in range(2):
        if dxl == 1:
            for key in x_copies:
                if key not in x_done:
                    from_x(*key)
        rows = pl.ds(dxl * GROUP, GROUP)
        head = qs[:, 0:W2]
        zero = jnp.zeros_like(head)
        narrow = ws[rows, 0:W2]
        level = dot_rows(narrow, jnp.where(column < W1, head, zero))
        lv[0, rows] = level
        level += dot_rows(narrow, jnp.where(column < W1, zero, head))
        lv[1, rows] = level
        level += dot_rows(ws[rows, W2:W3], qs[:, W2:W3])
        lv[2, rows] = level

        def score_step(index, total, rows=rows):
            cols = pl.ds(index * 1024, 1024)
            if not isinstance(index, int):
                cols = pl.ds(pl.multiple_of(index * 1024, 1024), 1024)
            return total + dot_rows(ws[rows, cols], qs[:, cols])

        level = score_step(1, level)
        arrived(y_copies[dxl])
        lv[3, rows] = lax.fori_loop(2, E // 1024, score_step, level)


    scales = [1.0 / math.sqrt(width) for width in WIDTHS]
    strips = [pl.ds(first, STRIP) for first in range(0, POOL, STRIP)]

    def tabulate(rows):
        rows = rows + [jnp.zeros((1, ROWS), F32)] * (8 - len(rows))
        return jnp.concatenate(rows, axis=0)

    def gather_terms(half):
        lanes = pl.ds(half * ROWS, ROWS)
        tops, sums, parts = [], [], []
        weight_sum = jnp.zeros((1, ROWS), F32)
        for strip in strips:
            weight_sum += jnp.sum(jnp.maximum(tt[strip, lanes], 0.0), axis=0, keepdims=True)
        for level in range(4):
            top = jnp.full((1, ROWS), -BIG, F32)
            for strip in strips:
                logits = jnp.where(
                    tt[strip, lanes] >= 0.0, lv[level, strip, lanes] * scales[level], -BIG
                )
                lv[level, strip, lanes] = logits
                top = jnp.maximum(top, jnp.max(logits, axis=0, keepdims=True))
            total = jnp.zeros((1, ROWS), F32)
            part = jnp.zeros((1, ROWS), F32)
            for strip in strips:
                shifted = lv[level, strip, lanes] - top
                weight = jnp.exp(shifted)
                lv[level, strip, lanes] = weight
                total += jnp.sum(weight, axis=0, keepdims=True)
                teacher = jnp.maximum(tt[strip, lanes], 0.0)
                part += jnp.sum(teacher * shifted, axis=0, keepdims=True)
            tops.append(top)
            sums.append(total)
            parts.append(part)
        st[half, 0] = tabulate(tops)
        st[half, 1] = tabulate(sums)
        st[half, 2] = tabulate(parts + [weight_sum])

    stats_copies = []
    for half in range(2):
        gather_terms(half)
        stats_copies.append(remote(st.at[half], sr.at[1 - half], sibling))

    loss_terms = []

    def finish_terms(half):
        lanes = pl.ds(half * ROWS, ROWS)
        top, top_other = st[half, 0], sr[half, 0]
        peak = jnp.maximum(top, top_other)
        fade, fade_other = jnp.exp(top - peak), jnp.exp(top_other - peak)
        total = st[half, 1] * fade + sr[half, 1] * fade_other
        factor = fade / total
        if half == 0:
            part, part_other = st[half, 2], sr[half, 2]
            weight, weight_other = part[4:5], part_other[4:5]
            part = part + weight * (top - peak) + part_other + weight_other * (top_other - peak)
            terms = jnp.log(total) * (weight + weight_other) - part
            loss_terms.append(jnp.sum(terms[:4], axis=0, keepdims=True))
        for strip in strips:
            teacher = jnp.maximum(tt[strip, lanes], 0.0)
            tail = None
            for level in (3, 2, 1, 0):
                student = lv[level, strip, lanes] * factor[level : level + 1]
                dlogit = (student - teacher) * scales[level]
                tail = dlogit if tail is None else dlogit + tail
                grid[level, strip, lanes] = tail.astype(BF16)

    for half in (1, 0):
        stats_copies[1 - half].wait_recv()
        finish_terms(half)


    pa, pab, pb, pbb, pc, pcb = (buf[k] for k in ("pa", "pab", "pb", "pbb", "pc", "pcb"))

    def dot_plain(a, b):
        return jnp.dot(a, b, preferred_element_type=F32)

    def keep(dxl, q, result):
        rounded = result.astype(BF16)
        xh_of, y_of = q // 4, q % 4
        for dz in range(NZ):
            top = slice(dz * SPAN, dz * SPAN + HALF)
            low = slice(dz * SPAN + HALF, (dz + 1) * SPAN)
            whole = slice(dz * SPAN, (dz + 1) * SPAN)
            pa[dz, dxl, q] = result[whole, :WA]
            pab[dz, dxl, q] = rounded[whole, :WA]
            at = (dz - FIRST_Z) % NZ
            pb[dxl, xh_of, y_of, at] = result[top, WA:]
            pbb[dxl, xh_of, y_of, at] = rounded[top, WA:]
            pc[y_of, dxl, xh_of, at] = result[low, WA:]
            pcb[y_of, dxl, xh_of, at] = rounded[low, WA:]

    ra, rax, ray, fa, ga = (buf[k] for k in ("ra", "rax", "ray", "fa", "ga"))
    ray_low, ga_low, rax_low = (buf[k] for k in ("ray_low", "ga_low", "rax_low"))

    def ring(way, step, dxl):
        dz = (way * (5 - step)) % NZ
        target = by_z[1 if way > 0 else NZ - 1]
        slot = ra.at[0 if way > 0 else 1, step - 1, dxl]
        if step == 1:
            rows = pl.ds(0 if way > 0 else HALF, HALF)
            return remote(pab.at[dz, dxl, :, rows], slot.at[:, rows], target)
        return remote(pab.at[dz, dxl], slot, target)

    def toward(d):
        return ((x + d) % NX) // 2

    rings = {}
    gb, gbb, rbx, rby = (buf[k] for k in ("gb", "gbb", "rbx", "rby"))
    gc, gcb, rcy, rcx = (buf[k] for k in ("gc", "gcb", "rcy", "rcx"))
    rbr, rcr = buf["rbr"], buf["rcr"]
    b_far, c_far, b_copies, c_copies = [], [], [[], []], [[], []]

    def opposite_b(chunk):
        part = pl.ds(*CHUNKS[chunk])
        b_far.append(
            [
                remote(pbb.at[0, toward(2), pl.ds(2 * h, 2), part], rbr.at[h, :, part], by_x[d])
                for h, d in ((0, 1), (1, 3))
            ]
        )

    def opposite_c(chunk):
        part = pl.ds(*CHUNKS[chunk])
        c_far.append(
            [
                remote(pcb.at[(y + 2) % NY, h, :, part], rcr.at[h, :, part], by_y[d])
                for h, d in ((0, 1), (1, 3))
            ]
        )

    def direct(chunk):
        part = pl.ds(*CHUNKS[chunk])
        for h, d in ((1, 1), (0, 3)):
            b_copies[chunk].append(
                remote(
                    pbb.at[1, toward(d), pl.ds(2 * h, 2), part],
                    rbx.at[1 - h, pl.ds(2 * h, 2), part],
                    by_x[d],
                )
            )
            c_copies[chunk].append(
                remote(pcb.at[(y + d) % NY, h, :, part], rcy.at[1 - h, h, :, part], by_y[d])
            )

    def relay(chunk):
        part = pl.ds(*CHUNKS[chunk])
        arrived(b_far[chunk])
        for h, d in ((0, 1), (1, 3)):
            half = pl.ds(2 * h, 2)
            total = pb[1, toward(d), half, part] + rbr[h, :, part].astype(F32)
            pbb[1, toward(d), half, part] = total.astype(BF16)
            b_copies[chunk].append(
                remote(pbb.at[1, toward(d), half, part], rbx.at[h, half, part], by_x[d])
            )
        arrived(c_far[chunk])
        for h, d in ((0, 1), (1, 3)):
            to = (y + d) % NY
            total = pc[to, h, :, part] + rcr[h, :, part].astype(F32)
            pcb[to, h, :, part] = total.astype(BF16)
            c_copies[chunk].append(
                remote(pcb.at[to, h, :, part], rcy.at[h, h, :, part], by_y[d])
            )

    for dxl in range(2):
        part = pl.ds(dxl * GROUP, GROUP)
        narrow = lax.broadcasted_iota(jnp.int32, (GROUP, W2), 1) < W1
        first = qs[:, 0:W2]
        first = jnp.where(
            narrow, dot_plain(grid[0, part], first), dot_plain(grid[1, part], first)
        )
        second = dot_plain(grid[2, part], qs[:, W2:BLOCK])
        keep(dxl, 0, jnp.concatenate([first, second], axis=1))
        keep(dxl, 1, dot_plain(grid[2, part], qs[:, BLOCK : 2 * BLOCK]))
        for q in range(2, 8):
            keep(dxl, q, dot_plain(grid[3, part], qs[:, q * BLOCK : (q + 1) * BLOCK]))
        for way in (1, -1):
            rings[way, dxl] = ring(way, 1, dxl)
        if dxl == 0:
            opposite_b(0)
    opposite_c(0)
    direct(0)

    diagonal = lax.broadcasted_iota(jnp.int32, (ROWS, LANES), 0) == lax.broadcasted_iota(
        jnp.int32, (ROWS, LANES), 1
    )
    entropy_row = jnp.sum(jnp.where(diagonal, entropy[0], 0.0), axis=0, keepdims=True)
    loss[...] = 4.0 * entropy_row + loss_terms[0]

    turned = buf["turned"]
    for level in range(4):
        turned[level] = grid[level].T

    def keep_query(cols, result):
        go[:, cols] = result[:ROWS]
        gs[:, cols] = result[ROWS:]

    first = ws[:, 0:W2]
    keep_query(
        slice(0, W2), jnp.where(column < W1, dot_plain(turned[0], first), dot_plain(turned[1], first))
    )
    keep_query(slice(W2, BLOCK), dot_plain(turned[2], ws[:, W2:BLOCK]))
    keep_query(slice(BLOCK, W3), dot_plain(turned[2], ws[:, BLOCK:W3]))

    def query_step(index, carry):
        cols = pl.ds(pl.multiple_of(index * BLOCK, BLOCK), BLOCK)
        keep_query(cols, dot_plain(turned[3], ws[:, cols]))
        return carry


    def ring_step(step):
        for dxl in range(2):
            for way in (1, -1):
                rings[way, dxl].wait_recv()
                dz = (way * (4 - step)) % NZ
                slot = ra.at[0 if way > 0 else 1, step - 1, dxl]
                rows = pl.ds(0, SPAN)
                if step == 1:
                    rows = pl.ds(0 if way > 0 else HALF, HALF)
                pab[dz, dxl, :, rows] = (pa[dz, dxl, :, rows] + slot[:, rows].astype(F32)).astype(
                    BF16
                )
                rings[way, dxl] = ring(way, step + 1, dxl)

    def ring_end():
        for dxl in range(2):
            rings[1, dxl].wait_recv()
            rings[-1, dxl].wait_recv()
            total = pa[0, dxl] + ra[0, 3, dxl].astype(F32) + ra[1, 3, dxl].astype(F32)
            fa[dxl] = total.reshape(2, 4, SPAN, WA)
        top, low = pl.ds(0, HALF), pl.ds(HALF, HALF)
        return (
            [remote(fa.at[d % 2, toward(d), :, top], rax.at[d - 1], by_x[d]) for d in (2, 1, 3)],
            [
                remote(fa.at[:, :, (y + d) % NY, low], ray_low.at[d - 1], by_y[d])
                for d in (2, 1, 3)
            ],
        )

    def three(own, parts):
        return own + parts[0].astype(F32) + parts[1].astype(F32) + parts[2].astype(F32)

    def b_second(chunk):
        part = pl.ds(*CHUNKS[chunk])
        arrived(b_copies[chunk])
        total = pb[0, xh, :, part] + rbx[0, :, part].astype(F32) + rbx[1, :, part].astype(F32)
        gb[:, part] = total
        gbb[:, part] = total.astype(BF16)
        return [
            remote(gbb.at[(y + d) % NY, part], rby.at[d - 1, part], by_y[d]) for d in (2, 1, 3)
        ]

    def c_second(chunk):
        part = pl.ds(*CHUNKS[chunk])
        arrived(c_copies[chunk])
        total = pc[y, :, :, part] + rcy[0, :, :, part].astype(F32)
        total += rcy[1, :, :, part].astype(F32)
        gc[:, :, part] = total
        gcb[:, :, part] = total.astype(BF16)
        return [
            remote(gcb.at[d % 2, toward(d), part], rcx.at[d - 1, part], by_x[d]) for d in (2, 1, 3)
        ]

    def third(chunk, total, wide, narrow, wide_in, narrow_in):
        start, count = CHUNKS[chunk]
        wide[pl.ds(start, count)] = total
        narrow[pl.ds(start, count)] = total.astype(BF16)
        copies = []
        for at in range(start, start + count):
            dz = (at + FIRST_Z) % NZ
            if dz in FAR:
                copies.append(remote(narrow.at[at], narrow_in.at[at], by_z[dz]))
            elif dz:
                copies.append(remote(wide.at[at], wide_in.at[at], by_z[dz]))
        return copies

    hb, hbb, rbz, rbzb = (buf[k] for k in ("hb", "hbb", "rbz", "rbzb"))
    hc, hcb, rcz, rczb = (buf[k] for k in ("hc", "hcb", "rcz", "rczb"))

    def b_third(chunk):
        part = pl.ds(*CHUNKS[chunk])
        arrived(b_next[chunk])
        return third(chunk, three(gb[y, part], rby[:, part]), hb, hbb, rbz, rbzb)

    def c_third(chunk):
        part = pl.ds(*CHUNKS[chunk])
        arrived(c_next[chunk])
        return third(chunk, three(gc[0, xh, part], rcx[:, part]), hc, hcb, rcz, rczb)

    b_next, c_next, last_copies = [None, None], [None, None], []
    relay(0)
    opposite_b(1)
    opposite_c(1)
    direct(1)
    ring_step(1)
    ring_step(2)
    lax.fori_loop(2, E // BLOCK, query_step, 0)
    query_copy = remote(gs, gr, sibling)
    b_next[0] = b_second(0)
    c_next[0] = c_second(0)
    ring_step(3)
    relay(1)
    last_copies += b_third(0)
    last_copies += c_third(0)
    a_copies = ring_end()
    b_next[1] = b_second(1)
    c_next[1] = c_second(1)
    arrived(a_copies[0])
    ga[...] = three(fa[0, xh, :, :HALF], rax)
    a_last = [remote(ga.at[(y + d) % NY], ray.at[d - 1], by_y[d]) for d in (2, 1, 3)]
    arrived(a_copies[1])
    ga_low[...] = three(fa[:, :, y, HALF:], ray_low)
    a_last += [
        remote(ga_low.at[d % 2, toward(d)], rax_low.at[d - 1], by_x[d]) for d in (2, 1, 3)
    ]
    last_copies += b_third(1)
    last_copies += c_third(1)
    query_copy.wait_recv()
    go[...] += gr[...]
    out_copy = local(go, grad_queries)
    arrived(a_last)
    ob = buf["ob"]
    ob[:HALF, :WA] = three(ga[y], ray)
    ob[HALF:, :WA] = three(ga_low[0, xh], rax_low)
    arrived(last_copies)
    at_home = (0 - FIRST_Z) % NZ
    total_b, total_c = hb[at_home], hc[at_home]
    for at in range(NZ):
        if (at + FIRST_Z) % NZ in FAR:
            total_b += rbzb[at].astype(F32)
            total_c += rczb[at].astype(F32)
        elif at != at_home:
            total_b += rbz[at]
            total_c += rcz[at]
    ob[:HALF, WA:] = total_b
    ob[HALF:, WA:] = total_c
    last = local(ob, grad_passages)
    for copy in sent:
        copy.wait_send()
    out_copy.wait()
    last.wait()


def main_call(queries, passages, candidates, scores):
    scratch = [pltpu.VMEM(shape, dtype) for shape, dtype in SCRATCH.values()]
    scratch += [
        pltpu.SemaphoreType.DMA((N_REMOTE,)),
        pltpu.SemaphoreType.DMA((N_REMOTE,)),
        pltpu.SemaphoreType.DMA((N_LOCAL,)),
    ]
    anywhere = pl.BlockSpec(memory_space=pl.ANY)
    return pl.pallas_call(
        main_kernel,
        out_shape=(
            jax.ShapeDtypeStruct((1, ROWS), F32),
            jax.ShapeDtypeStruct((ROWS, E), F32),
            jax.ShapeDtypeStruct((SPAN, BLOCK), F32),
        ),
        in_specs=[anywhere] * 4,
        out_specs=(pl.BlockSpec(memory_space=pltpu.VMEM), anywhere, anywhere),
        scratch_shapes=scratch,
        compiler_params=pltpu.CompilerParams(
            collective_id=0, has_side_effects=True, vmem_limit_bytes=60 * 2**20
        ),
        name="distill",
    )(queries, passages, candidates, scores)


def finish_kernel(*refs):
    sources, sinks, stages, sems = refs[:3], refs[3:6], refs[6:9], refs[9]
    pieces = [(0, pl.ds(first, PIECE)) for first in range(0, ROWS, PIECE)]
    pieces += [(1, slice(None)), (2, slice(None))]
    loads, stores = [], []
    for index, (which, rows) in enumerate(pieces):
        source, stage, sink = sources[which], stages[which], sinks[which]
        loads.append(pltpu.make_async_copy(source.at[rows], stage.at[rows], sems.at[0, index]))
        stores.append(pltpu.make_async_copy(stage.at[rows], sink.at[rows], sems.at[1, index]))
    for copy in loads:
        copy.start()
    for load, store in zip(loads, stores):
        load.wait()
        store.start()
    for copy in stores:
        copy.wait()


def finish(*arrays):
    anywhere = pl.BlockSpec(memory_space=pl.ANY)
    return pl.pallas_call(
        finish_kernel,
        out_shape=tuple(jax.ShapeDtypeStruct(a.shape, a.dtype) for a in arrays),
        in_specs=[anywhere] * 3,
        out_specs=(anywhere,) * 3,
        scratch_shapes=[pltpu.VMEM(a.shape, a.dtype) for a in arrays]
        + [pltpu.SemaphoreType.DMA((2, ROWS // PIECE + 2))],
        compiler_params=pltpu.CompilerParams(vmem_limit_bytes=60 * 2**20),
        name="finish",
    )(*arrays)


def shards(queries, passages, candidates, teacher_scores):
    loss, grad_queries, grad_passages = main_call(queries, passages, candidates, teacher_scores)
    grad_queries, grad_passages, loss = finish(grad_queries, grad_passages, loss)
    return (loss.reshape(ROWS), grad_queries, grad_passages)


def solution(mesh):
    return jax.shard_map(
        shards,
        mesh=mesh,
        in_specs=(
            P(("query", "passage"), None),
            P("passage", None),
            P(("query", "passage"), None),
            P(("query", "passage"), None),
        ),
        out_specs=(P(("query", "passage")), P(("query", "passage"), None), P("passage", "query")),
        check_vma=False,
    )
```
